32 devices in a mesh: groups: 2 (over x), src: 8 (over z, y), tgt: 2 (over core).
Axes of the slice: x: 2, y: 2, z: 4, core: 2. Of those that a mesh axis runs over, the one named last changes fastest.
Arguments:
- source_embed: bfloat16 [32768, 256], P(('groups', 'src')), parts along dimension 0, may hold values from -7 to 7
- target_embed: bfloat16 [32768, 256], P(('groups', 'tgt', 'src')), parts along dimension 0, may hold values from -6 to 6
- source_mass: float32 [32768], P(('groups', 'src')), parts along dimension 0, may hold values from 0.05 to 20
- target_mass: float32 [32768], P(('groups', 'tgt')), parts along dimension 0, may hold values from 0.05 to 20
- target_start: float32 [32768], P(('groups', 'tgt')), parts along dimension 0, may hold values from -3 to 11
- tile_list: int32 [16, 2, 2, 128], P(('groups', 'src'), 'tgt'), parts along dimension 0, may hold values from 0 to 63, as said below
- tile_count: int32 [16, 2], P(('groups', 'src'), 'tgt'), parts along dimension 0, may hold values from 25 to 128, as said below
Outputs:
- source_potential: float32 [32768], P(('groups', 'src')), parts along dimension 0
- target_potential: float32 [32768], P(('groups', 'tgt')), parts along dimension 0
The draws below stay inside these ranges and needn't reach their ends.
There are 2 independent parts, one for each index of `groups`. The reference program is written for one: setup_inputs(seed, part) draws one part's arguments, and reference() takes and returns one part's arrays. A program takes and returns all parts, laid end to end along the dimension named above; each array names one. Nothing has to cross between parts.
Inputs may be any that keep to these rules, and one draw needn't show every extreme that they name: `tile_list`: entry [s, t, 0, k] is a row block among the 16 blocks of src index s, entry [s, t, 1, k] a column block among the 64 blocks of tgt index t. The 128 tiles of a device are distinct; its first 16 are (r, (r + s * 16) mod 64) for r = 0 .. 15, so every row and every column of the whole has support. `tile_count`: number of live tiles of a device, which are the first ones of its list; in every part one device holds 128.
All inputs are finite; a program needn't handle non-finite values.
Results may differ from the reference program's by a relative error of at most 0.0004.
Values may be sent and summed in bfloat16 or wider, within the bound.
No kernel may reach another device: no remote copies, remote signals or barrier semaphores. Data moves between devices by JAX's collectives and lax.ppermute only.
A program may use at most 64 MiB of HBM per device.

```python
import math
import jax
import jax.numpy as jnp
from jax import lax

DE = 256
TILE = 128
RB = 16
CB = 64
ITERS = 2
TCAP = 128
NS = 16384
NT = 16384
N_SRC = 8
N_TGT = 2


def draw_source_embed(key, part):
    key = jax.random.fold_in(key, 11)
    values = jax.random.normal(key, (NS, DE), jnp.float32)
    return jnp.clip(values, -6.0, 6.0).astype(jnp.bfloat16)


def draw_target_start(key, part):
    key = jax.random.fold_in(key, 41)
    return jnp.clip(0.5 * jax.random.normal(key, (NT,), jnp.float32), -3.0, 3.0)


def draw_tile_list(key, part):
    key = jax.random.fold_in(key, 21)
    cells = RB * CB
    limit = 2 ** 30 // cells

    def one_device(device_key, src_index):
        marks = jax.random.randint(device_key, (cells,), 0, limit, dtype=jnp.int32)
        ranked = marks * cells + jnp.arange(cells, dtype=jnp.int32)
        cover_rows = jnp.arange(RB, dtype=jnp.int32)
        covered = cover_rows * CB + (cover_rows + src_index * RB) % CB
        matches = jnp.any(jnp.arange(cells, dtype=jnp.int32)[:, None] == covered[None, :], axis=1)
        ranked = jnp.where(matches, -1, ranked)
        chosen, unused_order = lax.top_k(ranked, TCAP - RB)
        picked = jnp.concatenate([covered, chosen % cells])
        return jnp.stack([picked // CB, picked % CB])
    device_keys = jax.random.split(key, N_SRC * N_TGT)
    src_index = jnp.repeat(jnp.arange(N_SRC, dtype=jnp.int32), N_TGT)
    lists = jax.vmap(one_device)(device_keys, src_index)
    return lists.reshape(N_SRC, N_TGT, 2, TCAP).astype(jnp.int32)


def draw_tile_count(key, part):
    key = jax.random.fold_in(key, 31)
    count_key, busy_key = jax.random.split(key)
    counts = jax.random.randint(count_key, (N_SRC * N_TGT,), TCAP // 5, TCAP // 2 + 1, dtype=jnp.int32)
    busiest = jax.random.randint(busy_key, (), 0, N_SRC * N_TGT, dtype=jnp.int32)
    counts = jnp.where(jnp.arange(N_SRC * N_TGT, dtype=jnp.int32) == busiest, TCAP, counts)
    return counts.reshape(N_SRC, N_TGT).astype(jnp.int32)


def block_scale(key, shape, cuts, smallest, high):
    def one(position, parts):
        heights = jax.random.uniform(jax.random.fold_in(jax.random.fold_in(key, 6), position), (parts,), jnp.float32, smallest / len(cuts), high / len(cuts))
        return jnp.repeat(jnp.exp(heights), shape[position] // parts).reshape((-1,) + (1,) * (len(shape) - position - 1))

    gain = one(*cuts[0])
    for cut in cuts[1:]:
        gain = gain * one(*cut)
    return gain


def noise(stream_key, dims, width, most, cuts=(), kind=jnp.bfloat16):
    entries = width * jax.random.normal(stream_key, dims, jnp.float32)
    if cuts:
        entries = entries * block_scale(stream_key, dims, cuts, -0.22, 0.18)
    return jnp.clip(entries, -most, most).astype(kind)


def setup_inputs(seed: int = 0, part: int = 0) -> dict:
    keys = jax.random.split(jax.random.key(seed), 8)
    own_keys = jax.random.split(jax.random.fold_in(keys[7], part), 8)
    source_embed = draw_source_embed(jax.random.fold_in(jax.random.fold_in(keys[7], part), 71), part)
    target_embed = noise(own_keys[1], (NT, DE), 1.0, 6.0, ((0, 16),))
    source_mass = jnp.clip(jnp.exp(math.log(20.0) - 5.9914645 * jax.random.uniform(own_keys[2], (NS,), jnp.float32) ** block_scale(own_keys[2], (NS,), ((0, 8),), -0.2, 0.2)), 0.05, 20.0)
    target_mass = jnp.clip(jnp.exp(math.log(20.0) - 5.9914645 * jax.random.uniform(own_keys[3], (NT,), jnp.float32) ** block_scale(own_keys[3], (NT,), ((0, 2),), -0.2, 0.2)), 0.05, 20.0)
    target_start = draw_target_start(jax.random.fold_in(jax.random.fold_in(keys[7], part), 71), part)
    tile_list = draw_tile_list(jax.random.fold_in(jax.random.fold_in(keys[7], part), 71), part)
    tile_count = draw_tile_count(jax.random.fold_in(jax.random.fold_in(keys[7], part), 71), part)
    return dict(source_embed=source_embed, target_embed=target_embed, source_mass=source_mass, target_mass=target_mass, target_start=target_start, tile_list=tile_list, tile_count=tile_count)


EPSILON = 0.05
FLOOR_VALUE = -1.0e30


def squared(tile_block):
    widened = tile_block.astype(jnp.float32)
    return jnp.sum(widened * widened, axis=-1)


def combine_stats(old_peak, old_summed, new_peak, new_summed):
    highest = jnp.maximum(old_peak, new_peak)
    return highest, old_summed * jnp.exp(old_peak - highest) + new_summed * jnp.exp(new_peak - highest)


def reference(source_embed, target_embed, source_mass, target_mass, target_start, tile_list, tile_count):
    row_blocks = NS // TILE
    col_blocks = NT // TILE
    source_tiles = source_embed.reshape(row_blocks, TILE, DE)
    target_tiles = target_embed.reshape(col_blocks, TILE, DE)
    source_norms = squared(source_tiles)
    target_norms = squared(target_tiles)
    src_shift = (jnp.arange(N_SRC, dtype=jnp.int32) * RB)[:, None, None]
    tgt_shift = (jnp.arange(N_TGT, dtype=jnp.int32) * CB)[None, :, None]
    slot_ids = jnp.arange(TCAP, dtype=jnp.int32)[None, None, :]
    rows_all = (tile_list[:, :, 0, :].astype(jnp.int32) + src_shift).reshape(-1)
    cols_all = (tile_list[:, :, 1, :].astype(jnp.int32) + tgt_shift).reshape(-1)
    live_slots = (slot_ids < tile_count[:, :, None].astype(jnp.int32)).reshape(-1)
    ordering = jnp.argsort(jnp.where(live_slots, 0, 1).astype(jnp.int32), stable=True)
    rows_all = rows_all[ordering].astype(jnp.int32)
    cols_all = cols_all[ordering].astype(jnp.int32)
    live_total = jnp.sum(live_slots.astype(jnp.int32))
    log_source = EPSILON * jnp.log(source_mass).reshape(row_blocks, TILE)
    log_target = EPSILON * jnp.log(target_mass).reshape(col_blocks, TILE)
    target_pot = target_start.reshape(col_blocks, TILE)

    def tile_cost(slot_number):
        row_block = rows_all[slot_number]
        col_block = cols_all[slot_number]
        products = jnp.dot(source_tiles[row_block], target_tiles[col_block].T, preferred_element_type=jnp.float32)
        cost_tile = (source_norms[row_block][:, None] + target_norms[col_block][None, :] - 2.0 * products) / DE
        return row_block, col_block, cost_tile

    source_pot = log_source
    for iteration in range(ITERS):
        def row_step(slot_number, running):
            row_block, col_block, cost_tile = tile_cost(slot_number)
            scores = (target_pot[col_block][None, :] - cost_tile) / EPSILON
            highest = jnp.max(scores, axis=1)
            summed = jnp.sum(jnp.exp(scores - highest[:, None]), axis=1)
            merged = combine_stats(running[0][row_block], running[1][row_block], highest, summed)
            return running[0].at[row_block].set(merged[0]), running[1].at[row_block].set(merged[1])

        row_start = (jnp.full((row_blocks, TILE), FLOOR_VALUE, jnp.float32), jnp.zeros((row_blocks, TILE), jnp.float32))
        row_peak, row_summed = lax.fori_loop(0, live_total, row_step, row_start)
        source_pot = log_source - EPSILON * (row_peak + jnp.log(row_summed))

        def column_step(slot_number, running):
            row_block, col_block, cost_tile = tile_cost(slot_number)
            scores = (source_pot[row_block][:, None] - cost_tile) / EPSILON
            highest = jnp.max(scores, axis=0)
            summed = jnp.sum(jnp.exp(scores - highest[None, :]), axis=0)
            merged = combine_stats(running[0][col_block], running[1][col_block], highest, summed)
            return running[0].at[col_block].set(merged[0]), running[1].at[col_block].set(merged[1])

        col_start = (jnp.full((col_blocks, TILE), FLOOR_VALUE, jnp.float32), jnp.zeros((col_blocks, TILE), jnp.float32))
        col_peak, col_summed = lax.fori_loop(0, live_total, column_step, col_start)
        target_pot = log_target - EPSILON * (col_peak + jnp.log(col_summed))
    return source_pot.reshape(NS), target_pot.reshape(NT)
```

```python
import math

import jax
import jax.numpy as jnp
from jax import lax
from jax.experimental import pallas as pl
from jax.experimental.pallas import tpu as pltpu
from jax.sharding import PartitionSpec as P

TILE = 128
EPSILON = 0.05
FLOOR = -1e30
UNROLL = 4
CHUNKS = 2
VMEM_LIMIT = 48 * 1024 * 1024


def hop(value, src_mask, tgt_mask=0):
    cores = lax.axis_size("tgt")
    total = lax.axis_size("src") * cores
    flip = src_mask * cores + tgt_mask
    return lax.ppermute(value, ("src", "tgt"), [(i, i ^ flip) for i in range(total)])


def half_norms(rows):
    wide = rows.astype(jnp.float32)
    return 0.5 * jnp.sum(wide * wide, axis=-1).reshape(-1, TILE)


def list_kernel(src_rows, col_blocks, meta, own, peer, rows, cols, total):
    upper = meta[0]
    slots = own.shape[1]

    def clear(i, carry):
        rows[i] = 0
        cols[i] = 0
        return carry

    lax.fori_loop(0, rows.shape[0], clear, 0)

    def scan(refs, shift):
        def step(k, found):
            col = refs[1, k] - upper * col_blocks
            rows[found] = refs[0, k] + shift * src_rows
            cols[found] = col
            return found + ((col >= 0) & (col < col_blocks)).astype(jnp.int32)

        return step

    found = lax.fori_loop(0, jnp.minimum(own[2, 0], slots), scan(own, upper), 0)
    found = lax.fori_loop(0, jnp.minimum(peer[2, 0], slots), scan(peer, 1 - upper), found)
    rows[found] = 0
    cols[found] = 0
    total[0] = found


def merge_logs(parts, scale):
    peak = parts[0]
    for part in parts[1:]:
        peak = jnp.maximum(peak, part)
    summed = sum(jnp.exp2((part - peak) * scale) for part in parts)
    return peak + jnp.log2(summed) / scale


def pass_kernel(
    scale, by_row, first, places, has_out, meta, rows, cols, total, *refs
):
    n_parts, n_src, n_tgt = places
    parts, refs = refs[:n_parts], refs[n_parts:]
    aux, refs = refs[0], refs[1:]
    src_pieces, refs = refs[: len(n_src)], refs[len(n_src) :]
    tgt_pieces, refs = refs[: len(n_tgt)], refs[len(n_tgt) :]
    out, refs = refs[0], refs[1:]
    if has_out:
        extra, refs = refs[0], refs[1:]
    src, tgt, spread, peaks, sums, sems = refs
    copies = []
    for ref, place in zip(src_pieces, n_src):
        start = pl.multiple_of(place(meta), ref.shape[0])
        copies.append((ref, src.at[pl.ds(start, ref.shape[0])]))
    for ref, place in zip(tgt_pieces, n_tgt):
        start = pl.multiple_of(place(meta), ref.shape[0])
        copies.append((ref, tgt.at[pl.ds(start, ref.shape[0])]))
    moves = [pltpu.make_async_copy(a, b, sems.at[i]) for i, (a, b) in enumerate(copies)]
    for move in moves:
        move.start()
    peaks[...] = jnp.full(peaks.shape, FLOOR, jnp.float32)
    sums[...] = jnp.zeros(sums.shape, jnp.float32)
    if first:
        potential = parts[0][...]
    else:
        potential = aux[...] - merge_logs([part[...] for part in parts], scale)
    if has_out:
        extra[...] = potential
    turned = jnp.transpose(potential)
    for block in range(potential.shape[0]):
        spread[block] = jnp.broadcast_to(turned[:, block : block + 1], (TILE, TILE))
    for move in moves:
        move.wait()
    known, reduced = (tgt, src) if by_row else (src, tgt)
    known_ids, reduced_ids = (cols, rows) if by_row else (rows, cols)
    dummy = peaks.shape[0] - 1
    count = total[0]

    def merge(carry):
        for place, peak, summed in carry:
            old_peak = peaks[place]
            old_sum = sums[place]
            top = jnp.maximum(old_peak, peak)
            peaks[place] = top
            sums[place] = old_sum * jnp.exp2((old_peak - top) * scale) + summed * jnp.exp2(
                (peak - top) * scale
            )

    def turn(index, carry):
        merge(carry)
        found = []
        for lane in range(UNROLL):
            slot = index * UNROLL + lane
            known_id, reduced_id = known_ids[slot], reduced_ids[slot]
            products = lax.dot_general(
                known[known_id],
                reduced[reduced_id],
                (((1,), (1,)), ((), ())),
                preferred_element_type=jnp.float32,
            )
            scores = (products + spread[known_id]).reshape(TILE // 8, 8, TILE)
            peak = jnp.max(scores, axis=0)
            summed = jnp.sum(jnp.exp2((scores - peak[None]) * scale), axis=0)
            found.append((jnp.where(slot < count, reduced_id, dummy), peak, summed))
        return tuple(found)

    nothing = tuple(
        (jnp.int32(dummy), jnp.full((8, TILE), FLOOR, jnp.float32), jnp.zeros((8, TILE), jnp.float32))
        for lane in range(UNROLL)
    )
    merge(lax.fori_loop(0, (count + UNROLL - 1) // UNROLL, turn, nothing))
    top = peaks[0:dummy]
    peak = jnp.max(top, axis=1)
    summed = jnp.sum(sums[0:dummy] * jnp.exp2((top - peak[:, None, :]) * scale), axis=1)
    live = summed > 0.0
    out[...] = jnp.where(live, peak + jnp.log2(jnp.where(live, summed, 1.0)) / scale, FLOOR)


def finish_kernel(scale, to_unit, parts_count, *refs):
    parts, (aux, norms, out) = refs[:parts_count], refs[parts_count:]
    potential = aux[...] - merge_logs([part[...] for part in parts], scale)
    out[...] = (potential + norms[...]) / to_unit


def shards(
    source_embed, target_embed, source_mass, target_mass, target_start, tile_list, tile_count
):
    width = source_embed.shape[1]
    shard_count = lax.axis_size("src")
    half = shard_count // 2
    src_index = lax.axis_index("src")
    core = lax.axis_index("tgt")
    upper = src_index // half
    unit = 2.0 / (width * EPSILON)
    scale = unit * math.log2(math.e)
    to_unit = 0.5 * width

    source_blocks = source_embed.reshape(-1, TILE, width)
    target_blocks = target_embed.reshape(-1, TILE, width)
    src_rows = source_blocks.shape[0]
    own_cols = target_blocks.shape[0]
    col_blocks = own_cols * half
    chunks = math.gcd(CHUNKS, own_cols)
    chunk = own_cols // chunks
    side = src_rows // lax.axis_size("tgt")
    pieces = math.gcd(CHUNKS, side)
    piece = side // pieces

    meta = jnp.stack([upper, core, src_index % half]).astype(jnp.int32)

    counts = jnp.broadcast_to(tile_count.reshape(1, 1), (1, tile_list.shape[3]))
    own_list = jnp.concatenate([tile_list[0, 0], counts], axis=0).astype(jnp.int32)
    log_source = (jnp.log(source_mass) / unit).reshape(src_rows, TILE)
    log_target = (jnp.log(target_mass) / unit).reshape(-1, TILE)

    held = {0: [target_blocks[i * chunk : (i + 1) * chunk] for i in range(chunks)]}
    for slot in range(1, half):
        low = slot & -slot
        held[slot] = [hop(part, low) for part in held[slot ^ low]]
    share = lax.dynamic_slice_in_dim(source_blocks, core * side, side)
    direct = [hop(share[i * piece : (i + 1) * piece], half) for i in range(pieces)]
    swapped = [hop(part, 0, 1) for part in direct]

    peer_list = hop(own_list, half)
    peer_log = hop(log_source, half)

    smem = pl.BlockSpec(memory_space=pltpu.SMEM)
    vmem = pl.BlockSpec(memory_space=pltpu.VMEM)
    slots = 2 * tile_list.shape[3] + UNROLL
    tiles = pl.pallas_call(
        lambda *refs: list_kernel(src_rows, col_blocks, *refs),
        out_shape=[jax.ShapeDtypeStruct((size,), jnp.int32) for size in (slots, slots, 1)],
        in_specs=[smem] * 3,
        out_specs=[smem] * 3,
        name="tile_lists",
    )(meta, own_list, peer_list)

    def pair(mine, theirs):
        return jnp.where(upper == 0, jnp.concatenate([mine, theirs]), jnp.concatenate([theirs, mine]))

    log_pair = pair(log_source, peer_log)
    log_half = lax.dynamic_slice_in_dim(log_target, upper * col_blocks, col_blocks)
    start_half = lax.dynamic_slice_in_dim(
        target_start.reshape(-1, TILE), upper * col_blocks, col_blocks
    )
    slot_norms = jnp.stack(
        [jnp.concatenate([half_norms(part) for part in held[slot]]) for slot in range(half)]
    )
    order = jnp.arange(half) ^ (src_index % half)
    target_norms = slot_norms[order].reshape(col_blocks, TILE)
    source_norms = half_norms(source_blocks)
    start = start_half * to_unit - target_norms

    src_pieces, src_places = [source_blocks], [lambda meta: meta[0] * src_rows]
    for turn, group in enumerate((direct, swapped)):
        for i, part in enumerate(group):
            src_pieces.append(part)
            src_places.append(
                lambda meta, turn=turn, i=i: (1 - meta[0]) * src_rows
                + jnp.abs(meta[1] - turn) * side
                + i * piece
            )
    tgt_pieces, tgt_places = [], []
    for slot in range(half):
        for i, part in enumerate(held[slot]):
            tgt_pieces.append(part)
            tgt_places.append(
                lambda meta, slot=slot, i=i: (meta[2] ^ slot) * own_cols + i * chunk
            )

    def run(by_row, first, parts, aux, has_out):
        known, reduced = (col_blocks, 2 * src_rows) if by_row else (2 * src_rows, col_blocks)
        out_shape = [jax.ShapeDtypeStruct((reduced, TILE), jnp.float32)]
        if has_out:
            out_shape.append(jax.ShapeDtypeStruct((known, TILE), jnp.float32))
        anywhere = pl.BlockSpec(memory_space=pl.ANY)
        count = len(src_pieces) + len(tgt_pieces)
        results = pl.pallas_call(
            lambda *refs: pass_kernel(
                scale, by_row, first, (len(parts), src_places, tgt_places), has_out, *refs
            ),
            out_shape=out_shape,
            in_specs=[smem] * 4 + [vmem] * (len(parts) + 1) + [anywhere] * count,
            out_specs=[vmem] * len(out_shape),
            scratch_shapes=[
                pltpu.VMEM((2 * src_rows, TILE, width), jnp.bfloat16),
                pltpu.VMEM((col_blocks, TILE, width), jnp.bfloat16),
                pltpu.VMEM((known, TILE, TILE), jnp.float32),
                pltpu.VMEM((reduced + 1, 8, TILE), jnp.float32),
                pltpu.VMEM((reduced + 1, 8, TILE), jnp.float32),
                pltpu.SemaphoreType.DMA((count,)),
            ],
            compiler_params=pltpu.CompilerParams(vmem_limit_bytes=VMEM_LIMIT),
            name="row_pass" if by_row else "column_pass",
        )(meta, *tiles, *parts, aux, *src_pieces, *tgt_pieces)
        return results

    def share_rows(part):
        return [part, hop(part, 0, 1), hop(part, half), hop(part, half, 1)]

    def share_columns(part):
        return [part] + [hop(part, mask) for mask in range(1, half)]

    rows = run(True, True, [start], start, False)[0]
    columns = run(False, False, share_rows(rows), log_pair, False)[0]
    rows = run(True, False, share_columns(columns), log_half, False)[0]
    columns, source_final = run(False, False, share_rows(rows), log_pair, True)
    gathered = share_columns(columns)
    target_final = pl.pallas_call(
        lambda *refs: finish_kernel(scale, to_unit, len(gathered), *refs),
        out_shape=jax.ShapeDtypeStruct((col_blocks, TILE), jnp.float32),
        in_specs=[vmem] * (len(gathered) + 2),
        out_specs=vmem,
        name="finish",
    )(*gathered, log_half, target_norms)
    target_pot = pair(target_final, hop(target_final, half))
    own_final = lax.dynamic_slice_in_dim(source_final, upper * src_rows, src_rows)
    source_pot = (own_final + source_norms) / to_unit
    return (source_pot.reshape(-1), target_pot.reshape(-1))


def solution(mesh):
    return jax.shard_map(
        shards,
        mesh=mesh,
        in_specs=(
            P(("groups", "src"), None),
            P(("groups", "tgt", "src"), None),
            P(("groups", "src")),
            P(("groups", "tgt")),
            P(("groups", "tgt")),
            P(("groups", "src"), "tgt", None, None),
            P(("groups", "src"), "tgt"),
        ),
        out_specs=(P(("groups", "src")), P(("groups", "tgt"))),
        check_vma=False,
    )
```

```python
import math

import jax
import jax.numpy as jnp
from jax import lax
from jax.experimental import pallas as pl
from jax.experimental.pallas import tpu as pltpu
from jax.sharding import PartitionSpec as P

TILE = 128
EPSILON = 0.05
FLOOR = -1e30
UNROLL = 8
CHUNKS = 2
VMEM_LIMIT = 6 * 1024 * 1024


def hop(value, src_mask, tgt_mask=0):
    cores = lax.axis_size("tgt")
    total = lax.axis_size("src") * cores
    flip = src_mask * cores + tgt_mask
    return lax.ppermute(value, ("src", "tgt"), [(i, i ^ flip) for i in range(total)])


def half_norms(rows):
    wide = rows.astype(jnp.float32)
    return 0.5 * jnp.sum(wide * wide, axis=-1).reshape(-1, TILE)


def list_kernel(src_rows, col_blocks, meta, own, peer, rows, cols, total):
    upper = meta[0]
    slots = own.shape[1]

    def clear(i, carry):
        rows[i] = 0
        cols[i] = 0
        return carry

    lax.fori_loop(0, rows.shape[0], clear, 0)

    def scan(refs, shift):
        def step(k, found):
            col = refs[1, k] - upper * col_blocks
            rows[found] = refs[0, k] + shift * src_rows
            cols[found] = col
            return found + ((col >= 0) & (col < col_blocks)).astype(jnp.int32)

        return step

    found = lax.fori_loop(0, jnp.minimum(own[2, 0], slots), scan(own, upper), 0)
    found = lax.fori_loop(0, jnp.minimum(peer[2, 0], slots), scan(peer, 1 - upper), found)
    rows[found] = 0
    cols[found] = 0
    total[0] = found


def merge_logs(parts, scale):
    peak = parts[0]
    for part in parts[1:]:
        peak = jnp.maximum(peak, part)
    summed = sum(jnp.exp2((part - peak) * scale) for part in parts)
    return peak + jnp.log2(summed) / scale


def product_kernel(places, meta, rows, cols, total, *refs):
    n_src, n_tgt = places
    src_pieces, refs = refs[: len(n_src)], refs[len(n_src) :]
    tgt_pieces, refs = refs[: len(n_tgt)], refs[len(n_tgt) :]
    by_col, by_row, src, tgt, sems = refs
    moves = []
    for pieces, places_of, held in ((src_pieces, n_src, src), (tgt_pieces, n_tgt, tgt)):
        for ref, place in zip(pieces, places_of):
            start = pl.multiple_of(place(meta), ref.shape[0])
            moves.append(
                pltpu.make_async_copy(ref, held.at[pl.ds(start, ref.shape[0])], sems.at[len(moves)])
            )
    for move in moves:
        move.start()
    for move in moves:
        move.wait()

    def turn(index, carry):
        for lane in range(UNROLL):
            slot = index * UNROLL + lane
            x, y = src[rows[slot]], tgt[cols[slot]]
            for left, right, out in ((y, x, by_col), (x, y, by_row)):
                out[slot] = lax.dot_general(
                    left, right, (((1,), (1,)), ((), ())), preferred_element_type=jnp.float32
                )
        return carry

    lax.fori_loop(0, (total[0] + UNROLL - 1) // UNROLL, turn, 0)


def pass_kernel(scale, n_parts, first, has_out, known_ids, reduced_ids, total, *refs):
    parts, refs = refs[:n_parts], refs[n_parts:]
    aux, products, out, refs = refs[0], refs[1], refs[2], refs[3:]
    if has_out:
        extra, refs = refs[0], refs[1:]
    spread, peaks, sums = refs
    peaks[...] = jnp.full(peaks.shape, FLOOR, jnp.float32)
    sums[...] = jnp.zeros(sums.shape, jnp.float32)
    if first:
        potential = parts[0][...]
    else:
        potential = aux[...] - merge_logs([part[...] for part in parts], scale)
    if has_out:
        extra[...] = potential
    turned = jnp.transpose(potential)
    for block in range(potential.shape[0]):
        spread[block] = jnp.broadcast_to(turned[:, block : block + 1], (TILE, TILE))
    dummy = peaks.shape[0] - 1
    count = total[0]

    def merge(carry):
        for place, peak, summed in carry:
            old_peak = peaks[place]
            old_sum = sums[place]
            top = jnp.maximum(old_peak, peak)
            peaks[place] = top
            sums[place] = old_sum * jnp.exp2((old_peak - top) * scale) + summed * jnp.exp2(
                (peak - top) * scale
            )

    def turn(index, carry):
        merge(carry)
        found = []
        for lane in range(UNROLL):
            slot = index * UNROLL + lane
            scores = (products[slot] + spread[known_ids[slot]]).reshape(TILE // 8, 8, TILE)
            peak = jnp.max(scores, axis=0)
            summed = jnp.sum(jnp.exp2((scores - peak[None]) * scale), axis=0)
            found.append((jnp.where(slot < count, reduced_ids[slot], dummy), peak, summed))
        return tuple(found)

    nothing = tuple(
        (jnp.int32(dummy), jnp.full((8, TILE), FLOOR, jnp.float32), jnp.zeros((8, TILE), jnp.float32))
        for lane in range(UNROLL)
    )
    merge(lax.fori_loop(0, (count + UNROLL - 1) // UNROLL, turn, nothing))
    top = peaks[0:dummy]
    peak = jnp.max(top, axis=1)
    summed = jnp.sum(sums[0:dummy] * jnp.exp2((top - peak[:, None, :]) * scale), axis=1)
    live = summed > 0.0
    out[...] = jnp.where(live, peak + jnp.log2(jnp.where(live, summed, 1.0)) / scale, FLOOR)


def finish_kernel(scale, to_unit, parts_count, *refs):
    parts, (aux, norms, out) = refs[:parts_count], refs[parts_count:]
    potential = aux[...] - merge_logs([part[...] for part in parts], scale)
    out[...] = (potential + norms[...]) / to_unit


def shards(
    source_embed, target_embed, source_mass, target_mass, target_start, tile_list, tile_count
):
    width = source_embed.shape[1]
    shard_count = lax.axis_size("src")
    half = shard_count // 2
    src_index = lax.axis_index("src")
    core = lax.axis_index("tgt")
    upper = src_index // half
    unit = 2.0 / (width * EPSILON)
    scale = unit * math.log2(math.e)
    to_unit = 0.5 * width

    source_blocks = source_embed.reshape(-1, TILE, width)
    target_blocks = target_embed.reshape(-1, TILE, width)
    src_rows = source_blocks.shape[0]
    own_cols = target_blocks.shape[0]
    col_blocks = own_cols * half
    chunks = math.gcd(CHUNKS, own_cols)
    chunk = own_cols // chunks
    side = src_rows // lax.axis_size("tgt")
    pieces = math.gcd(CHUNKS, side)
    piece = side // pieces

    meta = jnp.stack([upper, core, src_index % half]).astype(jnp.int32)

    counts = jnp.broadcast_to(tile_count.reshape(1, 1), (1, tile_list.shape[3]))
    own_list = jnp.concatenate([tile_list[0, 0], counts], axis=0).astype(jnp.int32)
    log_source = (jnp.log(source_mass) / unit).reshape(src_rows, TILE)
    log_target = (jnp.log(target_mass) / unit).reshape(-1, TILE)

    held = {0: [target_blocks[i * chunk : (i + 1) * chunk] for i in range(chunks)]}
    for slot in range(1, half):
        low = slot & -slot
        held[slot] = [hop(part, low) for part in held[slot ^ low]]
    share = lax.dynamic_slice_in_dim(source_blocks, core * side, side)
    direct = [hop(share[i * piece : (i + 1) * piece], half) for i in range(pieces)]
    swapped = [hop(part, 0, 1) for part in direct]

    peer_list = hop(own_list, half)
    peer_log = hop(log_source, half)

    smem = pl.BlockSpec(memory_space=pltpu.SMEM)
    vmem = pl.BlockSpec(memory_space=pltpu.VMEM)
    slots = 2 * tile_list.shape[3] + UNROLL
    tiles = pl.pallas_call(
        lambda *refs: list_kernel(src_rows, col_blocks, *refs),
        out_shape=[jax.ShapeDtypeStruct((size,), jnp.int32) for size in (slots, slots, 1)],
        in_specs=[smem] * 3,
        out_specs=[smem] * 3,
        compiler_params=pltpu.CompilerParams(vmem_limit_bytes=VMEM_LIMIT),
        name="tile_lists",
    )(meta, own_list, peer_list)

    def pair(mine, theirs):
        return jnp.where(upper == 0, jnp.concatenate([mine, theirs]), jnp.concatenate([theirs, mine]))

    log_pair = pair(log_source, peer_log)
    log_half = lax.dynamic_slice_in_dim(log_target, upper * col_blocks, col_blocks)
    start_half = lax.dynamic_slice_in_dim(
        target_start.reshape(-1, TILE), upper * col_blocks, col_blocks
    )
    slot_norms = jnp.stack(
        [jnp.concatenate([half_norms(part) for part in held[slot]]) for slot in range(half)]
    )
    order = jnp.arange(half) ^ (src_index % half)
    target_norms = slot_norms[order].reshape(col_blocks, TILE)
    source_norms = half_norms(source_blocks)
    start = start_half * to_unit - target_norms

    src_pieces, src_places = [source_blocks], [lambda meta: meta[0] * src_rows]
    for turn, group in enumerate((direct, swapped)):
        for i, part in enumerate(group):
            src_pieces.append(part)
            src_places.append(
                lambda meta, turn=turn, i=i: (1 - meta[0]) * src_rows
                + jnp.abs(meta[1] - turn) * side
                + i * piece
            )
    tgt_pieces, tgt_places = [], []
    for slot in range(half):
        for i, part in enumerate(held[slot]):
            tgt_pieces.append(part)
            tgt_places.append(
                lambda meta, slot=slot, i=i: (meta[2] ^ slot) * own_cols + i * chunk
            )

    anywhere = pl.BlockSpec(memory_space=pl.ANY)
    pieces_all = src_pieces + tgt_pieces
    by_col, by_row = pl.pallas_call(
        lambda *refs: product_kernel((src_places, tgt_places), *refs),
        out_shape=[jax.ShapeDtypeStruct((slots, TILE, TILE), jnp.float32)] * 2,
        in_specs=[smem] * 4 + [anywhere] * len(pieces_all),
        out_specs=[vmem] * 2,
        scratch_shapes=[
            pltpu.VMEM((2 * src_rows, TILE, width), jnp.bfloat16),
            pltpu.VMEM((col_blocks, TILE, width), jnp.bfloat16),
            pltpu.SemaphoreType.DMA((len(pieces_all),)),
        ],
        compiler_params=pltpu.CompilerParams(vmem_limit_bytes=VMEM_LIMIT),
        name="products",
    )(meta, *tiles, *pieces_all)

    def run(row_pass, first, parts, aux, has_out):
        known, reduced = (col_blocks, 2 * src_rows) if row_pass else (2 * src_rows, col_blocks)
        out_shape = [jax.ShapeDtypeStruct((reduced, TILE), jnp.float32)]
        if has_out:
            out_shape.append(jax.ShapeDtypeStruct((known, TILE), jnp.float32))
        rows, cols, total = tiles
        ids = (cols, rows) if row_pass else (rows, cols)
        return pl.pallas_call(
            lambda *refs: pass_kernel(scale, len(parts), first, has_out, *refs),
            out_shape=out_shape,
            in_specs=[smem] * 3 + [vmem] * (len(parts) + 2),
            out_specs=[vmem] * len(out_shape),
            scratch_shapes=[
                pltpu.VMEM((known, TILE, TILE), jnp.float32),
                pltpu.VMEM((reduced + 1, 8, TILE), jnp.float32),
                pltpu.VMEM((reduced + 1, 8, TILE), jnp.float32),
            ],
            compiler_params=pltpu.CompilerParams(vmem_limit_bytes=VMEM_LIMIT),
            name="row_pass" if row_pass else "column_pass",
        )(*ids, total, *parts, aux, by_col if row_pass else by_row)

    def share_rows(part):
        return [part, hop(part, 0, 1), hop(part, half), hop(part, half, 1)]

    def share_columns(part):
        return [part] + [hop(part, mask) for mask in range(1, half)]

    rows = run(True, True, [start], start, False)[0]
    columns = run(False, False, share_rows(rows), log_pair, False)[0]
    rows = run(True, False, share_columns(columns), log_half, False)[0]
    columns, source_final = run(False, False, share_rows(rows), log_pair, True)
    gathered = share_columns(columns)
    target_final = pl.pallas_call(
        lambda *refs: finish_kernel(scale, to_unit, len(gathered), *refs),
        out_shape=jax.ShapeDtypeStruct((col_blocks, TILE), jnp.float32),
        in_specs=[vmem] * (len(gathered) + 2),
        out_specs=vmem,
        compiler_params=pltpu.CompilerParams(vmem_limit_bytes=VMEM_LIMIT),
        name="finish",
    )(*gathered, log_half, target_norms)
    target_pot = pair(target_final, hop(target_final, half))
    own_final = lax.dynamic_slice_in_dim(source_final, upper * src_rows, src_rows)
    source_pot = (own_final + source_norms) / to_unit
    return (source_pot.reshape(-1), target_pot.reshape(-1))


def solution(mesh):
    return jax.shard_map(
        shards,
        mesh=mesh,
        in_specs=(
            P(("groups", "src"), None),
            P(("groups", "tgt", "src"), None),
            P(("groups", "src")),
            P(("groups", "tgt")),
            P(("groups", "tgt")),
            P(("groups", "src"), "tgt", None, None),
            P(("groups", "src"), "tgt"),
        ),
        out_specs=(P(("groups", "src")), P(("groups", "tgt"))),
        check_vma=False,
    )
```

```python
import math

import jax
import jax.numpy as jnp
from jax import lax
from jax.experimental import pallas as pl
from jax.experimental.pallas import tpu as pltpu
from jax.sharding import PartitionSpec as P

TILE = 128
EPSILON = 0.05
FLOOR = -1e30
UNROLL = 16
CHUNKS = 2
VMEM_LIMIT = 8 * 1024 * 1024


def hop(value, src_mask, tgt_mask=0):
    cores = lax.axis_size("tgt")
    total = lax.axis_size("src") * cores
    flip = src_mask * cores + tgt_mask
    return lax.ppermute(value, ("src", "tgt"), [(i, i ^ flip) for i in range(total)])


def half_norms(rows):
    wide = rows.astype(jnp.float32)
    return 0.5 * jnp.sum(wide * wide, axis=-1).reshape(-1, TILE)


def list_kernel(src_rows, col_blocks, slots, meta, own, peer, ids):
    upper = meta[0]
    listed = own.shape[1]

    def scan(refs, shift):
        live = refs[2, 0]

        def step(k, found):
            col = refs[1, k] - upper * col_blocks
            ids[found] = refs[0, k] + shift * src_rows
            ids[slots + found] = col
            keep = (col >= 0) & (col < col_blocks) & (k < live)
            return found + keep.astype(jnp.int32)

        return step

    found = lax.fori_loop(0, listed, scan(own, upper), 0, unroll=8)
    found = lax.fori_loop(0, listed, scan(peer, 1 - upper), found, unroll=8)
    for extra in range(UNROLL):
        ids[found + extra] = 0
        ids[slots + found + extra] = 0
    ids[2 * slots] = found


def merge_logs(parts):
    peak = parts[0]
    for part in parts[1:]:
        peak = jnp.maximum(peak, part)
    return peak + jnp.log2(sum(jnp.exp2(part - peak) for part in parts))


def spread_out(potential, spread):
    turned = jnp.transpose(potential)
    for block in range(potential.shape[0]):
        spread[block] = jnp.broadcast_to(turned[:, block : block + 1], (TILE, TILE))


def clear(peaks, sums):
    peaks[...] = jnp.full(peaks.shape, FLOOR, jnp.float32)
    sums[...] = jnp.zeros(sums.shape, jnp.float32)


def sweep(count, scores_of, known_of, reduced_of, spread, peaks, sums):
    dummy = peaks.shape[0] - 1

    def merge(carry):
        for place, peak, summed in carry:
            old_peak = peaks[place]
            old_sum = sums[place]
            top = jnp.maximum(old_peak, peak)
            peaks[place] = top
            sums[place] = old_sum * jnp.exp2(old_peak - top) + summed * jnp.exp2(peak - top)

    def turn(index, carry):
        merge(carry)
        fresh = []
        for lane in range(UNROLL):
            slot = index * UNROLL + lane
            scores = (scores_of(slot) + spread[known_of(slot)]).reshape(TILE // 8, 8, TILE)
            peak = jnp.max(scores, axis=0)
            summed = jnp.sum(jnp.exp2(scores - peak[None]), axis=0)
            fresh.append((jnp.where(slot < count, reduced_of(slot), dummy), peak, summed))
        return tuple(fresh)

    nothing = tuple(
        (jnp.int32(dummy), jnp.full((8, TILE), FLOOR, jnp.float32), jnp.zeros((8, TILE), jnp.float32))
        for lane in range(UNROLL)
    )
    merge(lax.fori_loop(0, (count + UNROLL - 1) // UNROLL, turn, nothing))


def log_sums(peaks, sums):
    top = peaks[0 : peaks.shape[0] - 1]
    peak = jnp.max(top, axis=1)
    summed = jnp.sum(sums[0 : top.shape[0]] * jnp.exp2(top - peak[:, None, :]), axis=1)
    live = summed > 0.0
    return jnp.where(live, peak + jnp.log2(jnp.where(live, summed, 1.0)), FLOOR)


def first_kernel(scale, slots, places, meta, ids_any, start, *refs):
    n_src, n_tgt, n_norm = places
    norm_parts, refs = refs[: len(n_norm)], refs[len(n_norm) :]
    src_pieces, refs = refs[: len(n_src)], refs[len(n_src) :]
    tgt_pieces, refs = refs[: len(n_tgt)], refs[len(n_tgt) :]
    out, by_col, src, tgt, norms, ids, spread, peaks, sums, sems = refs
    moves = [pltpu.make_async_copy(ids_any, ids, sems.at[0])]
    for pieces, places_of, held in ((src_pieces, n_src, src), (tgt_pieces, n_tgt, tgt)):
        for ref, place in zip(pieces, places_of):
            begin = pl.multiple_of(place(meta), ref.shape[0])
            moves.append(
                pltpu.make_async_copy(ref, held.at[pl.ds(begin, ref.shape[0])], sems.at[len(moves)])
            )
    for move in moves:
        move.start()
    clear(peaks, sums)
    for ref, place in zip(norm_parts, n_norm):
        begin = pl.multiple_of(place(meta), ref.shape[0])
        norms[pl.ds(begin, ref.shape[0])] = ref[...]
    spread_out(start[...] - scale * norms[...], spread)
    for move in moves:
        move.wait()

    def scores_of(slot):
        products = scale * lax.dot_general(
            tgt[ids[slots + slot]],
            src[ids[slot]],
            (((1,), (1,)), ((), ())),
            preferred_element_type=jnp.float32,
        )
        by_col[slot] = products
        return products

    sweep(
        ids[2 * slots],
        scores_of,
        lambda slot: ids[slots + slot],
        lambda slot: ids[slot],
        spread,
        peaks,
        sums,
    )
    out[...] = log_sums(peaks, sums)


def product_kernel(scale, slots, ids_any, src, tgt, by_row, ids, sem):
    move = pltpu.make_async_copy(ids_any, ids, sem)
    move.start()
    move.wait()

    def turn(index, carry):
        for lane in range(UNROLL):
            slot = index * UNROLL + lane
            by_row[slot] = scale * lax.dot_general(
                src[ids[slot]],
                tgt[ids[slots + slot]],
                (((1,), (1,)), ((), ())),
                preferred_element_type=jnp.float32,
            )
        return carry

    lax.fori_loop(0, (ids[2 * slots] + UNROLL - 1) // UNROLL, turn, 0)


def pass_kernel(slots, row_pass, n_parts, has_out, ids_any, *refs):
    parts, refs = refs[:n_parts], refs[n_parts:]
    mass, products, out, refs = refs[0], refs[1], refs[2], refs[3:]
    if has_out:
        extra, refs = refs[0], refs[1:]
    ids, spread, peaks, sums, sem = refs
    move = pltpu.make_async_copy(ids_any, ids, sem)
    move.start()
    clear(peaks, sums)
    potential = mass[...] - merge_logs([part[...] for part in parts])
    if has_out:
        extra[...] = potential
    spread_out(potential, spread)
    move.wait()
    known, reduced = (slots, 0) if row_pass else (0, slots)
    sweep(
        ids[2 * slots],
        lambda slot: products[slot],
        lambda slot: ids[known + slot],
        lambda slot: ids[reduced + slot],
        spread,
        peaks,
        sums,
    )
    out[...] = log_sums(peaks, sums)


def finish_kernel(scale, to_unit, parts_count, *refs):
    parts, (mass, norms, out) = refs[:parts_count], refs[parts_count:]
    potential = mass[...] - merge_logs([part[...] for part in parts])
    out[...] = (potential / scale + norms[...]) / to_unit


def shards(
    source_embed, target_embed, source_mass, target_mass, target_start, tile_list, tile_count
):
    width = source_embed.shape[1]
    shard_count = lax.axis_size("src")
    half = shard_count // 2
    src_index = lax.axis_index("src")
    core = lax.axis_index("tgt")
    upper = src_index // half
    scale = 2.0 / (width * EPSILON) * math.log2(math.e)
    to_unit = 0.5 * width

    source_blocks = source_embed.reshape(-1, TILE, width)
    target_blocks = target_embed.reshape(-1, TILE, width)
    src_rows = source_blocks.shape[0]
    own_cols = target_blocks.shape[0]
    col_blocks = own_cols * half
    chunks = math.gcd(CHUNKS, own_cols)
    chunk = own_cols // chunks
    side = src_rows // lax.axis_size("tgt")
    listed = tile_list.shape[3]
    slots = 2 * listed + UNROLL

    meta = jnp.stack([upper, core, src_index % half]).astype(jnp.int32)

    share = lax.dynamic_slice_in_dim(source_blocks, core * side, side)
    direct = hop(share, half)
    held = {0: [target_blocks]}
    for slot in range(1, half):
        low = slot & -slot
        before = held[slot ^ low]
        if slot == low and slot > 1:
            before = [target_blocks[i * chunk : (i + 1) * chunk] for i in range(chunks)]
        held[slot] = [hop(part, low) for part in before]
    swapped = hop(direct, 0, 1)

    mass = source_mass.reshape(src_rows, TILE)
    counts = jnp.broadcast_to(tile_count.reshape(1, 1), (1, listed))
    own_list = jnp.concatenate([tile_list[0, 0], counts], axis=0).astype(jnp.int32)
    facts = jnp.concatenate([own_list.astype(jnp.float32).reshape(-1, TILE), mass], axis=0)
    peer_facts = hop(facts, half)
    peer_list = peer_facts[:-src_rows].astype(jnp.int32).reshape(own_list.shape)
    peer_mass = peer_facts[-src_rows:]

    smem = pl.BlockSpec(memory_space=pltpu.SMEM)
    vmem = pl.BlockSpec(memory_space=pltpu.VMEM)
    anywhere = pl.BlockSpec(memory_space=pl.ANY)
    params = pltpu.CompilerParams(vmem_limit_bytes=VMEM_LIMIT)
    ids_size = -(-(2 * slots + 1) // 1024) * 1024
    ids = pl.pallas_call(
        lambda *refs: list_kernel(src_rows, col_blocks, slots, *refs),
        out_shape=jax.ShapeDtypeStruct((ids_size,), jnp.int32),
        in_specs=[smem] * 3,
        out_specs=smem,
        compiler_params=params,
        name="tile_lists",
    )(meta, own_list, peer_list)
    ids_scratch = pltpu.SMEM((ids_size,), jnp.int32)

    def pair(mine, theirs):
        return jnp.where(upper == 0, jnp.concatenate([mine, theirs]), jnp.concatenate([theirs, mine]))

    log_pair = jnp.log2(pair(mass, peer_mass))
    log_half = jnp.log2(
        lax.dynamic_slice_in_dim(target_mass.reshape(-1, TILE), upper * col_blocks, col_blocks)
    )
    start = (scale * to_unit) * lax.dynamic_slice_in_dim(
        target_start.reshape(-1, TILE), upper * col_blocks, col_blocks
    )
    source_norms = half_norms(source_blocks)

    src_pieces = [source_blocks, direct, swapped]
    src_places = [
        lambda meta: meta[0] * src_rows,
        lambda meta: (1 - meta[0]) * src_rows + meta[1] * side,
        lambda meta: (1 - meta[0]) * src_rows + (1 - meta[1]) * side,
    ]
    tgt_pieces, tgt_places, norm_parts = [], [], []
    for slot in range(half):
        parts = held[slot]
        step = own_cols // len(parts)
        for i, part in enumerate(parts):
            tgt_pieces.append(part)
            norm_parts.append(half_norms(part))
            tgt_places.append(
                lambda meta, slot=slot, begin=i * step: (meta[2] ^ slot) * own_cols + begin
            )

    def accumulators(known, reduced):
        return [
            ids_scratch,
            pltpu.VMEM((known, TILE, TILE), jnp.float32),
            pltpu.VMEM((reduced + 1, 8, TILE), jnp.float32),
            pltpu.VMEM((reduced + 1, 8, TILE), jnp.float32),
        ]

    moves = 1 + len(src_pieces) + len(tgt_pieces)
    rows, by_col, src, tgt, target_norms = pl.pallas_call(
        lambda *refs: first_kernel(scale, slots, (src_places, tgt_places, tgt_places), *refs),
        out_shape=[
            jax.ShapeDtypeStruct((2 * src_rows, TILE), jnp.float32),
            jax.ShapeDtypeStruct((slots, TILE, TILE), jnp.float32),
            jax.ShapeDtypeStruct((2 * src_rows, TILE, width), jnp.bfloat16),
            jax.ShapeDtypeStruct((col_blocks, TILE, width), jnp.bfloat16),
            jax.ShapeDtypeStruct((col_blocks, TILE), jnp.float32),
        ],
        in_specs=[smem, anywhere, vmem]
        + [vmem] * len(norm_parts)
        + [anywhere] * (len(src_pieces) + len(tgt_pieces)),
        out_specs=[vmem] * 5,
        scratch_shapes=accumulators(col_blocks, 2 * src_rows) + [pltpu.SemaphoreType.DMA((moves,))],
        compiler_params=params,
        name="first_row_pass",
    )(meta, ids, start, *norm_parts, *src_pieces, *tgt_pieces)

    by_row = pl.pallas_call(
        lambda *refs: product_kernel(scale, slots, *refs),
        out_shape=jax.ShapeDtypeStruct((slots, TILE, TILE), jnp.float32),
        in_specs=[anywhere, vmem, vmem],
        out_specs=vmem,
        scratch_shapes=[ids_scratch, pltpu.SemaphoreType.DMA],
        compiler_params=params,
        cost_estimate=pl.CostEstimate(
            flops=2 * 64 * TILE * TILE * width, bytes_accessed=8 * 1024 * 1024, transcendentals=0
        ),
        name="row_products",
    )(ids, src, tgt)

    def run(row_pass, parts, mass, has_out):
        known, reduced = (col_blocks, 2 * src_rows) if row_pass else (2 * src_rows, col_blocks)
        out_shape = [jax.ShapeDtypeStruct((reduced, TILE), jnp.float32)]
        if has_out:
            out_shape.append(jax.ShapeDtypeStruct((known, TILE), jnp.float32))
        return pl.pallas_call(
            lambda *refs: pass_kernel(slots, row_pass, len(parts), has_out, *refs),
            out_shape=out_shape,
            in_specs=[anywhere] + [vmem] * (len(parts) + 2),
            out_specs=[vmem] * len(out_shape),
            scratch_shapes=accumulators(known, reduced) + [pltpu.SemaphoreType.DMA],
            compiler_params=params,
            name="row_pass" if row_pass else "column_pass",
        )(ids, *parts, mass, by_col if row_pass else by_row)

    def share_rows(part):
        return [part, hop(part, half), hop(part, half, 1), hop(part, 0, 1)]

    def share_columns(part):
        return [part] + [hop(part, mask) for mask in range(1, half)]

    columns = run(False, share_rows(rows), log_pair, False)[0]
    rows = run(True, share_columns(columns), log_half, False)[0]
    columns, source_final = run(False, share_rows(rows), log_pair, True)
    gathered = share_columns(columns)
    target_final = pl.pallas_call(
        lambda *refs: finish_kernel(scale, to_unit, len(gathered), *refs),
        out_shape=jax.ShapeDtypeStruct((col_blocks, TILE), jnp.float32),
        in_specs=[vmem] * (len(gathered) + 2),
        out_specs=vmem,
        compiler_params=params,
        name="finish",
    )(*gathered, log_half, target_norms)
    target_pot = pair(target_final, hop(target_final, half))
    own_final = lax.dynamic_slice_in_dim(source_final, upper * src_rows, src_rows)
    source_pot = (own_final / scale + source_norms) / to_unit
    return (source_pot.reshape(-1), target_pot.reshape(-1))


def solution(mesh):
    return jax.shard_map(
        shards,
        mesh=mesh,
        in_specs=(
            P(("groups", "src"), None),
            P(("groups", "tgt", "src"), None),
            P(("groups", "src")),
            P(("groups", "tgt")),
            P(("groups", "tgt")),
            P(("groups", "src"), "tgt", None, None),
            P(("groups", "src"), "tgt"),
        ),
        out_specs=(P(("groups", "src")), P(("groups", "tgt"))),
        check_vma=False,
    )
```

```python
import math

import jax
import jax.numpy as jnp
from jax import lax
from jax.experimental import pallas as pl
from jax.experimental.pallas import tpu as pltpu
from jax.sharding import PartitionSpec as P

TILE = 128
EPSILON = 0.05
FLOOR = -1e30
MAKE_UNROLL = 16
READ_UNROLL = 8
PADDING = max(MAKE_UNROLL, READ_UNROLL)
VMEM_LIMIT = 4 * 1024 * 1024


def hop(value, src_mask, tgt_mask=0):
    cores = lax.axis_size("tgt")
    total = lax.axis_size("src") * cores
    flip = src_mask * cores + tgt_mask
    return lax.ppermute(value, ("src", "tgt"), [(i, i ^ flip) for i in range(total)])


def half_norms(rows):
    wide = rows.astype(jnp.float32)
    return 0.5 * jnp.sum(wide * wide, axis=-1).reshape(-1, TILE)


def share_kernel(side, source, first, second, share, sems):
    begin = lax.axis_index("tgt") * side
    move = pltpu.make_async_copy(source.at[pl.ds(begin, side)], share, sems.at[0])
    move.start()
    move.wait()


def list_kernel(half, src_rows, col_blocks, slots, own, peer, ids):
    upper = lax.axis_index("src") // half
    listed = own.shape[3]

    def scan(refs, shift):
        def step(k, found):
            col = refs[0, 0, 1, k] - upper * col_blocks
            ids[found] = refs[0, 0, 0, k] + shift * src_rows
            ids[slots + found] = col
            return found + ((col >= 0) & (col < col_blocks)).astype(jnp.int32)

        return step

    found = lax.fori_loop(0, listed, scan(own, upper), 0, unroll=8)
    found = lax.fori_loop(0, listed, scan(peer, 1 - upper), found, unroll=8)
    for extra in range(PADDING):
        ids[found + extra] = 0
        ids[slots + found + extra] = 0
    ids[2 * slots] = found


def merge_logs(parts):
    peak = parts[0]
    for part in parts[1:]:
        peak = jnp.maximum(peak, part)
    return peak + jnp.log2(sum(jnp.exp2(part - peak) for part in parts))


def spread_out(potential, spread):
    turned = jnp.transpose(potential)
    for block in range(potential.shape[0]):
        spread[block] = jnp.broadcast_to(turned[:, block : block + 1], (TILE, TILE))


def clear(peaks, sums):
    peaks[...] = jnp.full(peaks.shape, FLOOR, jnp.float32)
    sums[...] = jnp.zeros(sums.shape, jnp.float32)


def sweep(unroll, count, scores_of, known_of, reduced_of, spread, peaks, sums):
    dummy = peaks.shape[0] - 1

    def merge(carry):
        for place, peak, summed in carry:
            old_peak = peaks[place]
            old_sum = sums[place]
            top = jnp.maximum(old_peak, peak)
            peaks[place] = top
            sums[place] = old_sum * jnp.exp2(old_peak - top) + summed * jnp.exp2(peak - top)

    def turn(index, carry):
        merge(carry)
        fresh = []
        for lane in range(unroll):
            slot = index * unroll + lane
            scores = (scores_of(slot) + spread[known_of(slot)]).reshape(TILE // 8, 8, TILE)
            peak = jnp.max(scores, axis=0)
            summed = jnp.sum(jnp.exp2(scores - peak[None]), axis=0)
            fresh.append((jnp.where(slot < count, reduced_of(slot), dummy), peak, summed))
        return tuple(fresh)

    nothing = tuple(
        (jnp.int32(dummy), jnp.full((8, TILE), FLOOR, jnp.float32), jnp.zeros((8, TILE), jnp.float32))
        for lane in range(unroll)
    )
    merge(lax.fori_loop(0, (count + unroll - 1) // unroll, turn, nothing))


def log_sums(peaks, sums):
    top = peaks[0 : peaks.shape[0] - 1]
    peak = jnp.max(top, axis=1)
    summed = jnp.sum(sums[0 : top.shape[0]] * jnp.exp2(top - peak[:, None, :]), axis=1)
    live = summed > 0.0
    return jnp.where(live, peak + jnp.log2(jnp.where(live, summed, 1.0)), FLOOR)


def first_kernel(scale, half, slots, places, ids_any, start, mass, *refs):
    n_src, n_tgt, n_norm = places
    norm_parts, refs = refs[: len(n_norm)], refs[len(n_norm) :]
    src_pieces, refs = refs[: len(n_src)], refs[len(n_src) :]
    tgt_pieces, refs = refs[: len(n_tgt)], refs[len(n_tgt) :]
    out, by_col, src, tgt, norms, ids, spread, peaks, sums, sems = refs
    moves = [pltpu.make_async_copy(ids_any, ids, sems.at[0])]
    position = lax.axis_index("src")
    meta = (position // half, lax.axis_index("tgt"), position % half)
    for pieces, places_of, held in ((src_pieces, n_src, src), (tgt_pieces, n_tgt, tgt)):
        for ref, place in zip(pieces, places_of):
            begin = pl.multiple_of(place(meta), ref.shape[0])
            moves.append(
                pltpu.make_async_copy(ref, held.at[pl.ds(begin, ref.shape[0])], sems.at[len(moves)])
            )
    for move in moves:
        move.start()
    clear(peaks, sums)
    for ref, place in zip(norm_parts, n_norm):
        begin = pl.multiple_of(place(meta), ref.shape[0])
        norms[pl.ds(begin, ref.shape[0])] = ref[...]
    spread_out(start[...] - scale * norms[...], spread)
    for move in moves:
        move.wait()

    def scores_of(slot):
        products = scale * lax.dot_general(
            tgt[ids[slots + slot]],
            src[ids[slot]],
            (((1,), (1,)), ((), ())),
            preferred_element_type=jnp.float32,
        )
        by_col[slot] = products
        return products

    sweep(
        MAKE_UNROLL,
        ids[2 * slots],
        scores_of,
        lambda slot: ids[slots + slot],
        lambda slot: ids[slot],
        spread,
        peaks,
        sums,
    )
    own = mass.shape[0]
    out[0 : 2 * own] = log_sums(peaks, sums)
    out[2 * own :] = jnp.log2(mass[...])


def pass_kernel(scale, half, slots, row_pass, n_parts, makes, has_out, ids_any, *refs):
    parts, refs = refs[:n_parts], refs[n_parts:]
    mass, refs = refs[0], refs[1:]
    if makes:
        src, tgt, out, products, pair, refs = *refs[:5], refs[5:]
    else:
        products, out, refs = *refs[:2], refs[2:]
    if has_out:
        extra, refs = refs[0], refs[1:]
    ids, spread, peaks, sums, sem = refs
    move = pltpu.make_async_copy(ids_any, ids, sem)
    move.start()
    clear(peaks, sums)
    if makes:
        own = mass.shape[0] // 3
        upper = lax.axis_index("src") // half
        pair[pl.ds(pl.multiple_of(upper * own, own), own)] = mass[2 * own :]
        pair[pl.ds(pl.multiple_of((1 - upper) * own, own), own)] = parts[1][2 * own :]
        potential = pair[...] - merge_logs([part[0 : 2 * own] for part in parts])
    else:
        potential = mass[...] - merge_logs([part[...] for part in parts])
    if has_out:
        extra[...] = potential
    spread_out(potential, spread)
    move.wait()
    known, reduced = (slots, 0) if row_pass else (0, slots)

    def scores_of(slot):
        if makes:
            products[slot] = scale * lax.dot_general(
                src[ids[slot]],
                tgt[ids[slots + slot]],
                (((1,), (1,)), ((), ())),
                preferred_element_type=jnp.float32,
            )
        return products[slot]

    sweep(
        MAKE_UNROLL if makes else READ_UNROLL,
        ids[2 * slots],
        scores_of,
        lambda slot: ids[known + slot],
        lambda slot: ids[reduced + slot],
        spread,
        peaks,
        sums,
    )
    out[...] = log_sums(peaks, sums)


def finish_kernel(scale, to_unit, parts_count, *refs):
    parts, (mass, norms, out) = refs[:parts_count], refs[parts_count:]
    potential = mass[...] - merge_logs([part[...] for part in parts])
    out[...] = (potential / scale + norms[...]) / to_unit


def shards(
    source_embed, target_embed, source_mass, target_mass, target_start, tile_list, tile_count
):
    width = source_embed.shape[1]
    shard_count = lax.axis_size("src")
    half = shard_count // 2
    src_index = lax.axis_index("src")
    upper = src_index // half
    scale = 2.0 / (width * EPSILON) * math.log2(math.e)
    to_unit = 0.5 * width

    source_blocks = source_embed.reshape(-1, TILE, width)
    target_blocks = target_embed.reshape(-1, TILE, width)
    src_rows = source_blocks.shape[0]
    own_cols = target_blocks.shape[0]
    col_blocks = own_cols * half
    side = src_rows // lax.axis_size("tgt")
    listed = tile_list.shape[3]
    slots = 2 * listed + PADDING

    smem = pl.BlockSpec(memory_space=pltpu.SMEM)
    vmem = pl.BlockSpec(memory_space=pltpu.VMEM)
    anywhere = pl.BlockSpec(memory_space=pl.ANY)
    params = pltpu.CompilerParams(vmem_limit_bytes=VMEM_LIMIT)

    peer_list = hop(tile_list, half)
    peer_count = hop(tile_count, half)

    def live_list(tiles, count):
        live = lax.broadcasted_iota(jnp.int32, tiles.shape, 3) < count[0, 0]
        return jnp.where(live, tiles, -1)

    share = pl.pallas_call(
        lambda *refs: share_kernel(side, *refs),
        out_shape=jax.ShapeDtypeStruct((side, TILE, width), source_embed.dtype),
        in_specs=[anywhere] * 3,
        out_specs=vmem,
        scratch_shapes=[pltpu.SemaphoreType.DMA((1,))],
        compiler_params=params,
        name="outgoing",
    )(source_blocks, tile_count, tile_count)
    direct = hop(share, half)
    held = {0: target_blocks}
    for slot in range(1, half):
        low = slot & -slot
        held[slot] = hop(held[slot ^ low], low)
    swapped = hop(direct, 0, 1)
    ids_size = -(-(2 * slots + 1) // 1024) * 1024
    ids = pl.pallas_call(
        lambda *refs: list_kernel(half, src_rows, col_blocks, slots, *refs),
        out_shape=jax.ShapeDtypeStruct((ids_size,), jnp.int32),
        in_specs=[smem] * 2,
        out_specs=smem,
        compiler_params=params,
        name="tile_lists",
    )(live_list(tile_list, tile_count), live_list(peer_list, peer_count))
    ids_scratch = pltpu.SMEM((ids_size,), jnp.int32)

    log_half = jnp.log2(
        lax.dynamic_slice_in_dim(target_mass.reshape(-1, TILE), upper * col_blocks, col_blocks)
    )
    start = (scale * to_unit) * lax.dynamic_slice_in_dim(
        target_start.reshape(-1, TILE), upper * col_blocks, col_blocks
    )
    source_norms = half_norms(source_blocks)

    src_pieces = [source_blocks, direct, swapped]
    src_places = [
        lambda meta: meta[0] * src_rows,
        lambda meta: (1 - meta[0]) * src_rows + meta[1] * side,
        lambda meta: (1 - meta[0]) * src_rows + (1 - meta[1]) * side,
    ]
    tgt_pieces, tgt_places, norm_parts = [], [], []
    for slot in range(half):
        tgt_pieces.append(held[slot])
        norm_parts.append(half_norms(held[slot]))
        tgt_places.append(lambda meta, slot=slot: (meta[2] ^ slot) * own_cols)

    def accumulators(known, reduced):
        return [
            ids_scratch,
            pltpu.VMEM((known, TILE, TILE), jnp.float32),
            pltpu.VMEM((reduced + 1, 8, TILE), jnp.float32),
            pltpu.VMEM((reduced + 1, 8, TILE), jnp.float32),
        ]

    moves = 1 + len(src_pieces) + len(tgt_pieces)
    rows, by_col, src, tgt, target_norms = pl.pallas_call(
        lambda *refs: first_kernel(scale, half, slots, (src_places, tgt_places, tgt_places), *refs),
        out_shape=[
            jax.ShapeDtypeStruct((3 * src_rows, TILE), jnp.float32),
            jax.ShapeDtypeStruct((slots, TILE, TILE), jnp.float32),
            jax.ShapeDtypeStruct((2 * src_rows, TILE, width), jnp.bfloat16),
            jax.ShapeDtypeStruct((col_blocks, TILE, width), jnp.bfloat16),
            jax.ShapeDtypeStruct((col_blocks, TILE), jnp.float32),
        ],
        in_specs=[anywhere, vmem, vmem]
        + [vmem] * len(norm_parts)
        + [anywhere] * (len(src_pieces) + len(tgt_pieces)),
        out_specs=[vmem] * 5,
        scratch_shapes=accumulators(col_blocks, 2 * src_rows) + [pltpu.SemaphoreType.DMA((moves,))],
        compiler_params=params,
        name="first_row_pass",
    )(ids, start, source_mass.reshape(src_rows, TILE), *norm_parts, *src_pieces, *tgt_pieces)

    def run(row_pass, parts, mass, given, has_out):
        known, reduced = (col_blocks, 2 * src_rows) if row_pass else (2 * src_rows, col_blocks)
        makes = len(given) == 2
        out_shape = [jax.ShapeDtypeStruct((reduced, TILE), jnp.float32)]
        if makes:
            out_shape.append(jax.ShapeDtypeStruct((slots, TILE, TILE), jnp.float32))
            out_shape.append(jax.ShapeDtypeStruct((known, TILE), jnp.float32))
        if has_out:
            out_shape.append(jax.ShapeDtypeStruct((known, TILE), jnp.float32))
        return pl.pallas_call(
            lambda *refs: pass_kernel(scale, half, slots, row_pass, len(parts), makes, has_out, *refs),
            out_shape=out_shape,
            in_specs=[anywhere] + [vmem] * (len(parts) + 1 + len(given)),
            out_specs=[vmem] * len(out_shape),
            scratch_shapes=accumulators(known, reduced) + [pltpu.SemaphoreType.DMA],
            compiler_params=params,
            name="row_pass" if row_pass else "column_pass",
        )(ids, *parts, mass, *given)

    def share_rows(part):
        return [part, hop(part, half), hop(part, half, 1), hop(part, 0, 1)]

    def share_columns(part):
        return [part] + [hop(part, mask) for mask in range(1, half)]

    columns, by_row, log_pair = run(False, share_rows(rows), rows, [src, tgt], False)
    rows = run(True, share_columns(columns), log_half, [by_col], False)[0]
    columns, source_final = run(False, share_rows(rows), log_pair, [by_row], True)
    gathered = share_columns(columns)
    target_final = pl.pallas_call(
        lambda *refs: finish_kernel(scale, to_unit, len(gathered), *refs),
        out_shape=jax.ShapeDtypeStruct((col_blocks, TILE), jnp.float32),
        in_specs=[vmem] * (len(gathered) + 2),
        out_specs=vmem,
        compiler_params=params,
        name="finish",
    )(*gathered, log_half, target_norms)
    other = hop(target_final, half)
    target_pot = jnp.where(
        upper == 0, jnp.concatenate([target_final, other]), jnp.concatenate([other, target_final])
    )
    own_final = lax.dynamic_slice_in_dim(source_final, upper * src_rows, src_rows)
    source_pot = (own_final / scale + source_norms) / to_unit
    return (source_pot.reshape(-1), target_pot.reshape(-1))


def solution(mesh):
    return jax.shard_map(
        shards,
        mesh=mesh,
        in_specs=(
            P(("groups", "src"), None),
            P(("groups", "tgt", "src"), None),
            P(("groups", "src")),
            P(("groups", "tgt")),
            P(("groups", "tgt")),
            P(("groups", "src"), "tgt", None, None),
            P(("groups", "src"), "tgt"),
        ),
        out_specs=(P(("groups", "src")), P(("groups", "tgt"))),
        check_vma=False,
    )
```

```python
import math

import jax
import jax.numpy as jnp
from jax import lax
from jax.experimental import pallas as pl
from jax.experimental.pallas import tpu as pltpu
from jax.sharding import PartitionSpec as P

TILE = 128
EPSILON = 0.05
FLOOR = -1e30
MAKE_UNROLL = 20
READ_UNROLL = 8
PADDING = max(MAKE_UNROLL, READ_UNROLL)
VMEM_LIMIT = 3 * 1024 * 1024


def hop(value, src_mask, tgt_mask=0):
    cores = lax.axis_size("tgt")
    total = lax.axis_size("src") * cores
    flip = src_mask * cores + tgt_mask
    return lax.ppermute(value, ("src", "tgt"), [(i, i ^ flip) for i in range(total)])


def half_norms(rows):
    wide = rows.astype(jnp.float32)
    return 0.5 * jnp.sum(wide * wide, axis=-1).reshape(-1, TILE)


def share_kernel(side, source, share, sems):
    begin = lax.axis_index("tgt") * side
    move = pltpu.make_async_copy(source.at[pl.ds(begin, side)], share, sems.at[0])
    move.start()
    move.wait()


def list_kernel(half, src_rows, own_cols, slots, own, peer, ids):
    position = lax.axis_index("src")
    upper = position // half
    col_blocks = half * own_cols
    late = ((position % half) ^ (half - 1)) * own_cols
    listed = own.shape[3]

    def scan(refs, shift, wanted):
        def step(k, found):
            col = refs[0, 0, 1, k] - upper * col_blocks
            ids[found] = refs[0, 0, 0, k] + shift * src_rows
            ids[slots + found] = col
            return found + wanted(col).astype(jnp.int32)

        return step

    def is_late(col):
        return (col >= late) & (col < late + own_cols)

    def is_here(col):
        return (col >= 0) & (col < col_blocks)

    early = scan(own, upper, lambda col: is_here(col) & jnp.logical_not(is_late(col)))
    found = lax.fori_loop(0, listed, early, 0, unroll=8)
    ids[2 * slots + 1] = found
    found = lax.fori_loop(0, listed, scan(own, upper, is_late), found, unroll=8)
    found = lax.fori_loop(0, listed, scan(peer, 1 - upper, is_here), found, unroll=8)
    for extra in range(PADDING):
        ids[found + extra] = 0
        ids[slots + found + extra] = 0
    ids[2 * slots] = found


def merge_logs(parts):
    peak = parts[0]
    for part in parts[1:]:
        peak = jnp.maximum(peak, part)
    return peak + jnp.log2(sum(jnp.exp2(part - peak) for part in parts))


def spread_out(potential, spread, begin=0):
    turned = jnp.transpose(potential)
    for block in range(potential.shape[0]):
        spread[begin + block] = jnp.broadcast_to(turned[:, block : block + 1], (TILE, TILE))


def clear(peaks, sums):
    peaks[...] = jnp.full(peaks.shape, FLOOR, jnp.float32)
    sums[...] = jnp.zeros(sums.shape, jnp.float32)


def sweep(unroll, begin, count, scores_of, known_of, reduced_of, spread, peaks, sums):
    dummy = peaks.shape[0] - 1

    def merge(carry):
        for place, peak, summed in carry:
            old_peak = peaks[place]
            old_sum = sums[place]
            top = jnp.maximum(old_peak, peak)
            peaks[place] = top
            sums[place] = old_sum * jnp.exp2(old_peak - top) + summed * jnp.exp2(peak - top)

    def turn(index, carry):
        merge(carry)
        fresh = []
        for lane in range(unroll):
            slot = begin + index * unroll + lane
            scores = (scores_of(slot) + spread[known_of(slot)]).reshape(TILE // 8, 8, TILE)
            peak = jnp.max(scores, axis=0)
            summed = jnp.sum(jnp.exp2(scores - peak[None]), axis=0)
            fresh.append((jnp.where(slot < count, reduced_of(slot), dummy), peak, summed))
        return tuple(fresh)

    nothing = tuple(
        (jnp.int32(dummy), jnp.full((8, TILE), FLOOR, jnp.float32), jnp.zeros((8, TILE), jnp.float32))
        for lane in range(unroll)
    )
    merge(lax.fori_loop(0, (count - begin + unroll - 1) // unroll, turn, nothing))


def log_sums(peaks, sums):
    top = peaks[0 : peaks.shape[0] - 1]
    peak = jnp.max(top, axis=1)
    summed = jnp.sum(sums[0 : top.shape[0]] * jnp.exp2(top - peak[:, None, :]), axis=1)
    live = summed > 0.0
    return jnp.where(live, peak + jnp.log2(jnp.where(live, summed, 1.0)), FLOOR)


def gather_parts(meta, groups, sems, first_sem):
    moves = []
    for pieces, places_of, whole in groups:
        for ref, place in zip(pieces, places_of):
            begin = pl.multiple_of(place(meta), ref.shape[0])
            moves.append(
                pltpu.make_async_copy(
                    ref, whole.at[pl.ds(begin, ref.shape[0])], sems.at[first_sem + len(moves)]
                )
            )
    return moves


def first_kernel(scale, half, slots, late, places, ids_any, start, *refs):
    n_src, n_tgt = places
    norm_parts, refs = refs[: len(n_tgt)], refs[len(n_tgt) :]
    src_pieces, refs = refs[: len(n_src)], refs[len(n_src) :]
    tgt_pieces, refs = refs[: len(n_tgt)], refs[len(n_tgt) :]
    if late:
        mass, out, refs = refs[0], refs[8], refs[9:]
    by_col, src, tgt, norms, spread, peaks, sums, ids, sems = refs
    position = lax.axis_index("src")
    meta = (position // half, lax.axis_index("tgt"), position % half)
    moves = [pltpu.make_async_copy(ids_any, ids, sems.at[0])]
    moves += gather_parts(meta, ((src_pieces, n_src, src), (tgt_pieces, n_tgt, tgt)), sems, 1)
    for move in moves:
        move.start()
    if not late:
        clear(peaks, sums)
    for ref, place in zip(norm_parts, n_tgt):
        begin = pl.multiple_of(place(meta), ref.shape[0])
        norms[pl.ds(begin, ref.shape[0])] = ref[...]
        spread_out(start[pl.ds(begin, ref.shape[0])] - scale * ref[...], spread, begin)
    for move in moves:
        move.wait()

    def scores_of(slot):
        products = scale * lax.dot_general(
            tgt[ids[slots + slot]],
            src[ids[slot]],
            (((1,), (1,)), ((), ())),
            preferred_element_type=jnp.float32,
        )
        by_col[jnp.minimum(slot, by_col.shape[0] - 1)] = products
        return products

    sweep(
        MAKE_UNROLL,
        ids[2 * slots + 1] if late else 0,
        ids[2 * slots] if late else ids[2 * slots + 1],
        scores_of,
        lambda slot: ids[slots + slot],
        lambda slot: ids[slot],
        spread,
        peaks,
        sums,
    )
    if late:
        own = mass.shape[0]
        out[0 : 2 * own] = log_sums(peaks, sums)
        out[2 * own :] = jnp.log2(mass[...])


def pass_kernel(scale, half, slots, row_pass, n_parts, makes, has_out, ids_any, *refs):
    parts, refs = refs[:n_parts], refs[n_parts:]
    mass, refs = refs[0], refs[1:]
    if makes:
        src, tgt, out, products, pair, refs = *refs[:5], refs[5:]
    else:
        products, out, refs = *refs[:2], refs[2:]
    if has_out:
        extra, refs = refs[0], refs[1:]
    ids, spread, peaks, sums, sem = refs
    move = pltpu.make_async_copy(ids_any, ids, sem)
    move.start()
    clear(peaks, sums)
    if makes:
        own = mass.shape[0] // 3
        upper = lax.axis_index("src") // half
        pair[pl.ds(pl.multiple_of(upper * own, own), own)] = mass[2 * own :]
        pair[pl.ds(pl.multiple_of((1 - upper) * own, own), own)] = parts[1][2 * own :]
        potential = pair[...] - merge_logs([part[0 : 2 * own] for part in parts])
    else:
        potential = mass[...] - merge_logs([part[...] for part in parts])
    if has_out:
        extra[...] = potential
    spread_out(potential, spread)
    move.wait()
    known, reduced = (slots, 0) if row_pass else (0, slots)

    def scores_of(slot):
        if not makes:
            return products[jnp.minimum(slot, products.shape[0] - 1)]
        made = scale * lax.dot_general(
            src[ids[slot]],
            tgt[ids[slots + slot]],
            (((1,), (1,)), ((), ())),
            preferred_element_type=jnp.float32,
        )
        products[jnp.minimum(slot, products.shape[0] - 1)] = made
        return made

    sweep(
        MAKE_UNROLL if makes else READ_UNROLL,
        0,
        ids[2 * slots],
        scores_of,
        lambda slot: ids[known + slot],
        lambda slot: ids[reduced + slot],
        spread,
        peaks,
        sums,
    )
    out[...] = log_sums(peaks, sums)


def finish_kernel(scale, to_unit, parts_count, *refs):
    parts, (mass, norms, out) = refs[:parts_count], refs[parts_count:]
    potential = mass[...] - merge_logs([part[...] for part in parts])
    out[...] = (potential / scale + norms[...]) / to_unit


def shards(
    source_embed, target_embed, source_mass, target_mass, target_start, tile_list, tile_count
):
    width = source_embed.shape[1]
    shard_count = lax.axis_size("src")
    half = shard_count // 2
    src_index = lax.axis_index("src")
    upper = src_index // half
    scale = 2.0 / (width * EPSILON) * math.log2(math.e)
    to_unit = 0.5 * width

    source_blocks = source_embed.reshape(-1, TILE, width)
    target_blocks = target_embed.reshape(-1, TILE, width)
    src_rows = source_blocks.shape[0]
    own_cols = target_blocks.shape[0]
    col_blocks = own_cols * half
    side = src_rows // lax.axis_size("tgt")
    listed = tile_list.shape[3]
    slots = 2 * listed + PADDING

    smem = pl.BlockSpec(memory_space=pltpu.SMEM)
    vmem = pl.BlockSpec(memory_space=pltpu.VMEM)
    anywhere = pl.BlockSpec(memory_space=pl.ANY)
    params = pltpu.CompilerParams(vmem_limit_bytes=VMEM_LIMIT)

    peer_list = hop(tile_list, half)
    peer_count = hop(tile_count, half)

    def live_list(tiles, count):
        live = lax.broadcasted_iota(jnp.int32, tiles.shape, 3) < count[0, 0]
        return jnp.where(live, tiles, -1)

    share = pl.pallas_call(
        lambda *refs: share_kernel(side, *refs),
        out_shape=jax.ShapeDtypeStruct((side, TILE, width), source_embed.dtype),
        in_specs=[anywhere],
        out_specs=vmem,
        scratch_shapes=[pltpu.SemaphoreType.DMA((1,))],
        compiler_params=params,
        name="outgoing",
    )(source_blocks)
    direct = hop(share, half)
    held = {0: target_blocks}
    for slot in range(1, half):
        low = slot & -slot
        held[slot] = hop(held[slot ^ low], low)
    ids_size = -(-(2 * slots + 2) // 1024) * 1024
    ids = pl.pallas_call(
        lambda *refs: list_kernel(half, src_rows, own_cols, slots, *refs),
        out_shape=jax.ShapeDtypeStruct((ids_size,), jnp.int32),
        in_specs=[smem] * 2,
        out_specs=smem,
        compiler_params=params,
        name="tile_lists",
    )(live_list(tile_list, tile_count), live_list(peer_list, peer_count))
    ids_scratch = pltpu.SMEM((ids_size,), jnp.int32)

    log_half = jnp.log2(
        lax.dynamic_slice_in_dim(target_mass.reshape(-1, TILE), upper * col_blocks, col_blocks)
    )
    start = (scale * to_unit) * lax.dynamic_slice_in_dim(
        target_start.reshape(-1, TILE), upper * col_blocks, col_blocks
    )
    source_norms = half_norms(source_blocks)

    src_pieces = [source_blocks]
    src_places = [
        lambda meta: meta[0] * src_rows,
        lambda meta: (1 - meta[0]) * src_rows + meta[1] * side,
        lambda meta: (1 - meta[0]) * src_rows + (1 - meta[1]) * side,
    ]
    tgt_pieces, tgt_places, norm_parts = [], [], []
    for slot in range(half):
        tgt_pieces.append(held[slot])
        norm_parts.append(half_norms(held[slot]))
        tgt_places.append(lambda meta, slot=slot: (meta[2] ^ slot) * own_cols)

    def accumulators(known, reduced):
        return [
            ids_scratch,
            pltpu.VMEM((known, TILE, TILE), jnp.float32),
            pltpu.VMEM((reduced + 1, 8, TILE), jnp.float32),
            pltpu.VMEM((reduced + 1, 8, TILE), jnp.float32),
        ]

    shared = [
        jax.ShapeDtypeStruct((2 * listed + 1, TILE, TILE), jnp.float32),
        jax.ShapeDtypeStruct((2 * src_rows, TILE, width), jnp.bfloat16),
        jax.ShapeDtypeStruct((col_blocks, TILE, width), jnp.bfloat16),
        jax.ShapeDtypeStruct((col_blocks, TILE), jnp.float32),
        jax.ShapeDtypeStruct((col_blocks, TILE, TILE), jnp.float32),
        jax.ShapeDtypeStruct((2 * src_rows + 1, 8, TILE), jnp.float32),
        jax.ShapeDtypeStruct((2 * src_rows + 1, 8, TILE), jnp.float32),
    ]

    def first(late, given):
        srcs = slice(1, None) if late else slice(0, 1)
        tgts = slice(half - 1, None) if late else slice(0, half - 1)
        pieces = src_pieces[srcs] + tgt_pieces[tgts]
        norms = norm_parts[tgts]
        inputs = [ids, start, *norms, *pieces, *given]
        out_shape = shared
        if late:
            out_shape = [jax.ShapeDtypeStruct((3 * src_rows, TILE), jnp.float32)] + shared
        return pl.pallas_call(
            lambda *refs: first_kernel(
                scale, half, slots, late, (src_places[srcs], tgt_places[tgts]), *refs
            ),
            out_shape=out_shape,
            in_specs=[anywhere] + [vmem] * (1 + len(norms)) + [anywhere] * len(pieces) + [vmem] * len(given),
            out_specs=[vmem] * len(out_shape),
            scratch_shapes=[ids_scratch, pltpu.SemaphoreType.DMA((1 + len(pieces),))],
            input_output_aliases=(
                {len(inputs) - len(shared) + i: 1 + i for i in range(len(shared))} if late else {}
            ),
            compiler_params=params,
            name="late_row_pass" if late else "early_row_pass",
        )(*inputs)

    kept = list(first(False, []))
    direct, kept[5] = lax.optimization_barrier((direct, kept[5]))
    src_pieces[1:] = [direct, hop(direct, 0, 1)]
    rows, by_col, src, tgt, target_norms = first(
        True, [source_mass.reshape(src_rows, TILE), *kept]
    )[:5]

    def run(row_pass, parts, mass, given, has_out):
        known, reduced = (col_blocks, 2 * src_rows) if row_pass else (2 * src_rows, col_blocks)
        makes = len(given) == 2
        out_shape = [jax.ShapeDtypeStruct((reduced, TILE), jnp.float32)]
        if makes:
            out_shape.append(jax.ShapeDtypeStruct((2 * listed + 1, TILE, TILE), jnp.float32))
            out_shape.append(jax.ShapeDtypeStruct((known, TILE), jnp.float32))
        if has_out:
            out_shape.append(jax.ShapeDtypeStruct((known, TILE), jnp.float32))
        return pl.pallas_call(
            lambda *refs: pass_kernel(scale, half, slots, row_pass, len(parts), makes, has_out, *refs),
            out_shape=out_shape,
            in_specs=[anywhere] + [vmem] * (len(parts) + 1 + len(given)),
            out_specs=[vmem] * len(out_shape),
            scratch_shapes=accumulators(known, reduced) + [pltpu.SemaphoreType.DMA],
            compiler_params=params,
            name="row_pass" if row_pass else "column_pass",
        )(ids, *parts, mass, *given)

    def share_rows(part):
        return [part, hop(part, half), hop(part, half, 1), hop(part, 0, 1)]

    def share_columns(part):
        return [part] + [hop(part, mask) for mask in range(1, half)]

    columns, by_row, log_pair = run(False, share_rows(rows), rows, [src, tgt], False)
    rows = run(True, share_columns(columns), log_half, [by_col], False)[0]
    columns, source_final = run(False, share_rows(rows), log_pair, [by_row], True)
    gathered = share_columns(columns)
    target_final = pl.pallas_call(
        lambda *refs: finish_kernel(scale, to_unit, len(gathered), *refs),
        out_shape=jax.ShapeDtypeStruct((col_blocks, TILE), jnp.float32),
        in_specs=[vmem] * (len(gathered) + 2),
        out_specs=vmem,
        compiler_params=params,
        name="finish",
    )(*gathered, log_half, target_norms)
    other = hop(target_final, half)
    target_pot = jnp.where(
        upper == 0, jnp.concatenate([target_final, other]), jnp.concatenate([other, target_final])
    )
    own_final = lax.dynamic_slice_in_dim(source_final, upper * src_rows, src_rows)
    source_pot = (own_final / scale + source_norms) / to_unit
    return (source_pot.reshape(-1), target_pot.reshape(-1))


def solution(mesh):
    return jax.shard_map(
        shards,
        mesh=mesh,
        in_specs=(
            P(("groups", "src"), None),
            P(("groups", "tgt", "src"), None),
            P(("groups", "src")),
            P(("groups", "tgt")),
            P(("groups", "tgt")),
            P(("groups", "src"), "tgt", None, None),
            P(("groups", "src"), "tgt"),
        ),
        out_specs=(P(("groups", "src")), P(("groups", "tgt"))),
        check_vma=False,
    )
```

```python
import math

import jax
import jax.numpy as jnp
from jax import lax
from jax.experimental import pallas as pl
from jax.experimental.pallas import tpu as pltpu
from jax.sharding import PartitionSpec as P

TILE = 128
EPSILON = 0.05
FLOOR = -1e30
MAKE_UNROLL = 20
READ_UNROLL = 8
TURN_UNROLL = 16
PADDING = max(MAKE_UNROLL, READ_UNROLL)
VMEM_LIMIT = 3 * 1024 * 1024


def hop(value, src_mask, tgt_mask=0):
    cores = lax.axis_size("tgt")
    total = lax.axis_size("src") * cores
    flip = src_mask * cores + tgt_mask
    return lax.ppermute(value, ("src", "tgt"), [(i, i ^ flip) for i in range(total)])


def half_norms(rows):
    wide = rows.astype(jnp.float32)
    return 0.5 * jnp.sum(wide * wide, axis=-1).reshape(-1, TILE)


def share_kernel(side, source, share, sems):
    begin = lax.axis_index("tgt") * side
    move = pltpu.make_async_copy(source.at[pl.ds(begin, side)], share, sems.at[0])
    move.start()
    move.wait()


def list_kernel(half, src_rows, own_cols, slots, own, peer, ids):
    position = lax.axis_index("src")
    upper = position // half
    col_blocks = half * own_cols
    late = ((position % half) ^ (half - 1)) * own_cols
    listed = own.shape[3]

    def scan(refs, shift, wanted):
        def step(k, found):
            col = refs[0, 0, 1, k] - upper * col_blocks
            ids[found] = refs[0, 0, 0, k] + shift * src_rows
            ids[slots + found] = col
            return found + wanted(col).astype(jnp.int32)

        return step

    def is_late(col):
        return (col >= late) & (col < late + own_cols)

    def is_here(col):
        return (col >= 0) & (col < col_blocks)

    early = scan(own, upper, lambda col: is_here(col) & jnp.logical_not(is_late(col)))
    found = lax.fori_loop(0, listed, early, 0, unroll=8)
    ids[2 * slots + 1] = found
    found = lax.fori_loop(0, listed, scan(own, upper, is_late), found, unroll=8)
    found = lax.fori_loop(0, listed, scan(peer, 1 - upper, is_here), found, unroll=8)
    for extra in range(PADDING):
        ids[found + extra] = 0
        ids[slots + found + extra] = 0
    ids[2 * slots] = found


def merge_logs(parts):
    peak = parts[0]
    for part in parts[1:]:
        peak = jnp.maximum(peak, part)
    return peak + jnp.log2(sum(jnp.exp2(part - peak) for part in parts))


def spread_out(potential, spread, begin=0):
    turned = jnp.transpose(potential)
    for block in range(potential.shape[0]):
        spread[begin + block] = jnp.broadcast_to(turned[:, block : block + 1], (TILE, TILE))


def clear(peaks, sums):
    peaks[...] = jnp.full(peaks.shape, FLOOR, jnp.float32)
    sums[...] = jnp.zeros(sums.shape, jnp.float32)


def sweep(unroll, begin, count, scores_of, known_of, reduced_of, spread, peaks, sums):
    dummy = peaks.shape[0] - 1

    def merge(carry):
        for place, peak, summed in carry:
            old_peak = peaks[place]
            old_sum = sums[place]
            top = jnp.maximum(old_peak, peak)
            peaks[place] = top
            sums[place] = old_sum * jnp.exp2(old_peak - top) + summed * jnp.exp2(peak - top)

    def turn(index, carry):
        merge(carry)
        fresh = []
        for lane in range(unroll):
            slot = begin + index * unroll + lane
            scores = (scores_of(slot) + spread[known_of(slot)]).reshape(TILE // 8, 8, TILE)
            peak = jnp.max(scores, axis=0)
            summed = jnp.sum(jnp.exp2(scores - peak[None]), axis=0)
            fresh.append((jnp.where(slot < count, reduced_of(slot), dummy), peak, summed))
        return tuple(fresh)

    nothing = tuple(
        (jnp.int32(dummy), jnp.full((8, TILE), FLOOR, jnp.float32), jnp.zeros((8, TILE), jnp.float32))
        for lane in range(unroll)
    )
    merge(lax.fori_loop(0, (count - begin + unroll - 1) // unroll, turn, nothing))


def log_sums(peaks, sums):
    top = peaks[0 : peaks.shape[0] - 1]
    peak = jnp.max(top, axis=1)
    summed = jnp.sum(sums[0 : top.shape[0]] * jnp.exp2(top - peak[:, None, :]), axis=1)
    live = summed > 0.0
    return jnp.where(live, peak + jnp.log2(jnp.where(live, summed, 1.0)), FLOOR)


def gather_parts(meta, groups, sems, first_sem):
    moves = []
    for pieces, places_of, whole in groups:
        for ref, place in zip(pieces, places_of):
            begin = pl.multiple_of(place(meta), ref.shape[0])
            moves.append(
                pltpu.make_async_copy(
                    ref, whole.at[pl.ds(begin, ref.shape[0])], sems.at[first_sem + len(moves)]
                )
            )
    return moves


def first_kernel(scale, half, slots, late, places, ids_any, start, *refs):
    n_src, n_tgt = places
    norm_parts, refs = refs[: len(n_tgt)], refs[len(n_tgt) :]
    src_pieces, refs = refs[: len(n_src)], refs[len(n_src) :]
    tgt_pieces, refs = refs[: len(n_tgt)], refs[len(n_tgt) :]
    if late:
        mass, out, refs = refs[0], refs[8], refs[9:]
    by_col, src, tgt, norms, spread, peaks, sums, ids, sems = refs
    position = lax.axis_index("src")
    meta = (position // half, lax.axis_index("tgt"), position % half)
    moves = [pltpu.make_async_copy(ids_any, ids, sems.at[0])]
    moves += gather_parts(meta, ((src_pieces, n_src, src), (tgt_pieces, n_tgt, tgt)), sems, 1)
    for move in moves:
        move.start()
    if not late:
        clear(peaks, sums)
    for ref, place in zip(norm_parts, n_tgt):
        begin = pl.multiple_of(place(meta), ref.shape[0])
        norms[pl.ds(begin, ref.shape[0])] = ref[...]
        spread_out(start[pl.ds(begin, ref.shape[0])] - scale * ref[...], spread, begin)
    for move in moves:
        move.wait()

    def scores_of(slot):
        products = scale * lax.dot_general(
            tgt[ids[slots + slot]],
            src[ids[slot]],
            (((1,), (1,)), ((), ())),
            preferred_element_type=jnp.float32,
        )
        by_col[jnp.minimum(slot, by_col.shape[0] - 1)] = products
        return products

    sweep(
        MAKE_UNROLL,
        ids[2 * slots + 1] if late else 0,
        ids[2 * slots] if late else ids[2 * slots + 1],
        scores_of,
        lambda slot: ids[slots + slot],
        lambda slot: ids[slot],
        spread,
        peaks,
        sums,
    )
    if late:
        own = mass.shape[0]
        out[0 : 2 * own] = log_sums(peaks, sums)
        out[2 * own :] = jnp.log2(mass[...])


def pass_kernel(half, slots, row_pass, n_parts, makes, has_out, ids_any, *refs):
    parts, refs = refs[:n_parts], refs[n_parts:]
    mass, refs = refs[0], refs[1:]
    if makes:
        turned, out, products, pair, refs = *refs[:4], refs[4:]
    else:
        products, out, refs = *refs[:2], refs[2:]
    if has_out:
        extra, refs = refs[0], refs[1:]
    ids, spread, peaks, sums, sem = refs
    move = pltpu.make_async_copy(ids_any, ids, sem)
    move.start()
    clear(peaks, sums)
    if makes:
        own = mass.shape[0] // 3
        upper = lax.axis_index("src") // half
        pair[pl.ds(pl.multiple_of(upper * own, own), own)] = mass[2 * own :]
        pair[pl.ds(pl.multiple_of((1 - upper) * own, own), own)] = parts[1][2 * own :]
        potential = pair[...] - merge_logs([part[0 : 2 * own] for part in parts])
    else:
        potential = mass[...] - merge_logs([part[...] for part in parts])
    if has_out:
        extra[...] = potential
    spread_out(potential, spread)
    move.wait()
    known, reduced = (slots, 0) if row_pass else (0, slots)

    def scores_of(slot):
        if not makes:
            return products[jnp.minimum(slot, products.shape[0] - 1)]
        place = jnp.minimum(slot, products.shape[0] - 1)
        made = jnp.transpose(turned[place])
        products[place] = made
        return made

    sweep(
        TURN_UNROLL if makes else READ_UNROLL,
        0,
        ids[2 * slots],
        scores_of,
        lambda slot: ids[known + slot],
        lambda slot: ids[reduced + slot],
        spread,
        peaks,
        sums,
    )
    out[...] = log_sums(peaks, sums)


def finish_kernel(scale, to_unit, parts_count, *refs):
    parts, (mass, norms, out) = refs[:parts_count], refs[parts_count:]
    potential = mass[...] - merge_logs([part[...] for part in parts])
    out[...] = (potential / scale + norms[...]) / to_unit


def shards(
    source_embed, target_embed, source_mass, target_mass, target_start, tile_list, tile_count
):
    width = source_embed.shape[1]
    shard_count = lax.axis_size("src")
    half = shard_count // 2
    src_index = lax.axis_index("src")
    upper = src_index // half
    scale = 2.0 / (width * EPSILON) * math.log2(math.e)
    to_unit = 0.5 * width

    source_blocks = source_embed.reshape(-1, TILE, width)
    target_blocks = target_embed.reshape(-1, TILE, width)
    src_rows = source_blocks.shape[0]
    own_cols = target_blocks.shape[0]
    col_blocks = own_cols * half
    side = src_rows // lax.axis_size("tgt")
    listed = tile_list.shape[3]
    slots = 2 * listed + PADDING

    smem = pl.BlockSpec(memory_space=pltpu.SMEM)
    vmem = pl.BlockSpec(memory_space=pltpu.VMEM)
    anywhere = pl.BlockSpec(memory_space=pl.ANY)
    params = pltpu.CompilerParams(vmem_limit_bytes=VMEM_LIMIT)

    peer_list = hop(tile_list, half)
    peer_count = hop(tile_count, half)

    def live_list(tiles, count):
        live = lax.broadcasted_iota(jnp.int32, tiles.shape, 3) < count[0, 0]
        return jnp.where(live, tiles, -1)

    share = pl.pallas_call(
        lambda *refs: share_kernel(side, *refs),
        out_shape=jax.ShapeDtypeStruct((side, TILE, width), source_embed.dtype),
        in_specs=[anywhere],
        out_specs=vmem,
        scratch_shapes=[pltpu.SemaphoreType.DMA((1,))],
        compiler_params=params,
        name="outgoing",
    )(source_blocks)
    direct = hop(share, half)
    held = {0: target_blocks}
    for slot in range(1, half):
        low = slot & -slot
        held[slot] = hop(held[slot ^ low], low)
    ids_size = -(-(2 * slots + 2) // 1024) * 1024
    ids = pl.pallas_call(
        lambda *refs: list_kernel(half, src_rows, own_cols, slots, *refs),
        out_shape=jax.ShapeDtypeStruct((ids_size,), jnp.int32),
        in_specs=[smem] * 2,
        out_specs=smem,
        compiler_params=params,
        name="tile_lists",
    )(live_list(tile_list, tile_count), live_list(peer_list, peer_count))
    ids_scratch = pltpu.SMEM((ids_size,), jnp.int32)

    log_half = jnp.log2(
        lax.dynamic_slice_in_dim(target_mass.reshape(-1, TILE), upper * col_blocks, col_blocks)
    )
    start = (scale * to_unit) * lax.dynamic_slice_in_dim(
        target_start.reshape(-1, TILE), upper * col_blocks, col_blocks
    )
    source_norms = half_norms(source_blocks)

    src_pieces = [source_blocks]
    src_places = [
        lambda meta: meta[0] * src_rows,
        lambda meta: (1 - meta[0]) * src_rows + meta[1] * side,
        lambda meta: (1 - meta[0]) * src_rows + (1 - meta[1]) * side,
    ]
    tgt_pieces, tgt_places, norm_parts = [], [], []
    for slot in range(half):
        tgt_pieces.append(held[slot])
        norm_parts.append(half_norms(held[slot]))
        tgt_places.append(lambda meta, slot=slot: (meta[2] ^ slot) * own_cols)

    def accumulators(known, reduced):
        return [
            ids_scratch,
            pltpu.VMEM((known, TILE, TILE), jnp.float32),
            pltpu.VMEM((reduced + 1, 8, TILE), jnp.float32),
            pltpu.VMEM((reduced + 1, 8, TILE), jnp.float32),
        ]

    shared = [
        jax.ShapeDtypeStruct((2 * listed + 1, TILE, TILE), jnp.float32),
        jax.ShapeDtypeStruct((2 * src_rows, TILE, width), jnp.bfloat16),
        jax.ShapeDtypeStruct((col_blocks, TILE, width), jnp.bfloat16),
        jax.ShapeDtypeStruct((col_blocks, TILE), jnp.float32),
        jax.ShapeDtypeStruct((col_blocks, TILE, TILE), jnp.float32),
        jax.ShapeDtypeStruct((2 * src_rows + 1, 8, TILE), jnp.float32),
        jax.ShapeDtypeStruct((2 * src_rows + 1, 8, TILE), jnp.float32),
    ]

    def first(late, given):
        srcs = slice(1, None) if late else slice(0, 1)
        tgts = slice(half - 1, None) if late else slice(0, half - 1)
        pieces = src_pieces[srcs] + tgt_pieces[tgts]
        norms = norm_parts[tgts]
        inputs = [ids, start, *norms, *pieces, *given]
        out_shape = shared
        if late:
            out_shape = [jax.ShapeDtypeStruct((3 * src_rows, TILE), jnp.float32)] + shared
        return pl.pallas_call(
            lambda *refs: first_kernel(
                scale, half, slots, late, (src_places[srcs], tgt_places[tgts]), *refs
            ),
            out_shape=out_shape,
            in_specs=[anywhere] + [vmem] * (1 + len(norms)) + [anywhere] * len(pieces) + [vmem] * len(given),
            out_specs=[vmem] * len(out_shape),
            scratch_shapes=[ids_scratch, pltpu.SemaphoreType.DMA((1 + len(pieces),))],
            input_output_aliases=(
                {len(inputs) - len(shared) + i: 1 + i for i in range(len(shared))} if late else {}
            ),
            compiler_params=params,
            name="late_row_pass" if late else "early_row_pass",
        )(*inputs)

    kept = list(first(False, []))
    direct, kept[5] = lax.optimization_barrier((direct, kept[5]))
    src_pieces[1:] = [direct, hop(direct, 0, 1)]
    rows, by_col, src, tgt, target_norms = first(
        True, [source_mass.reshape(src_rows, TILE), *kept]
    )[:5]

    def run(row_pass, parts, mass, products, makes, has_out):
        known, reduced = (col_blocks, 2 * src_rows) if row_pass else (2 * src_rows, col_blocks)
        out_shape = [jax.ShapeDtypeStruct((reduced, TILE), jnp.float32)]
        if makes:
            out_shape.append(jax.ShapeDtypeStruct((2 * listed + 1, TILE, TILE), jnp.float32))
            out_shape.append(jax.ShapeDtypeStruct((known, TILE), jnp.float32))
        if has_out:
            out_shape.append(jax.ShapeDtypeStruct((known, TILE), jnp.float32))
        return pl.pallas_call(
            lambda *refs: pass_kernel(half, slots, row_pass, len(parts), makes, has_out, *refs),
            out_shape=out_shape,
            in_specs=[anywhere] + [vmem] * (len(parts) + 2),
            out_specs=[vmem] * len(out_shape),
            scratch_shapes=accumulators(known, reduced) + [pltpu.SemaphoreType.DMA],
            compiler_params=params,
            name="row_pass" if row_pass else "column_pass",
        )(ids, *parts, mass, products)

    def share_rows(part):
        return [part, hop(part, half), hop(part, half, 1), hop(part, 0, 1)]

    def share_columns(part):
        return [part] + [hop(part, mask) for mask in range(1, half)]

    columns, by_row, log_pair = run(False, share_rows(rows), rows, by_col, True, False)
    rows = run(True, share_columns(columns), log_half, by_col, False, False)[0]
    columns, source_final = run(False, share_rows(rows), log_pair, by_row, False, True)
    gathered = share_columns(columns)
    target_final = pl.pallas_call(
        lambda *refs: finish_kernel(scale, to_unit, len(gathered), *refs),
        out_shape=jax.ShapeDtypeStruct((col_blocks, TILE), jnp.float32),
        in_specs=[vmem] * (len(gathered) + 2),
        out_specs=vmem,
        compiler_params=params,
        name="finish",
    )(*gathered, log_half, target_norms)
    other = hop(target_final, half)
    target_pot = jnp.where(
        upper == 0, jnp.concatenate([target_final, other]), jnp.concatenate([other, target_final])
    )
    own_final = lax.dynamic_slice_in_dim(source_final, upper * src_rows, src_rows)
    source_pot = (own_final / scale + source_norms) / to_unit
    return (source_pot.reshape(-1), target_pot.reshape(-1))


def solution(mesh):
    return jax.shard_map(
        shards,
        mesh=mesh,
        in_specs=(
            P(("groups", "src"), None),
            P(("groups", "tgt", "src"), None),
            P(("groups", "src")),
            P(("groups", "tgt")),
            P(("groups", "tgt")),
            P(("groups", "src"), "tgt", None, None),
            P(("groups", "src"), "tgt"),
        ),
        out_specs=(P(("groups", "src")), P(("groups", "tgt"))),
        check_vma=False,
    )
```

```python
import math

import jax
import jax.numpy as jnp
from jax import lax
from jax.experimental import pallas as pl
from jax.experimental.pallas import tpu as pltpu
from jax.sharding import PartitionSpec as P

TILE = 128
EPSILON = 0.05
FLOOR = -1e30
MAKE_UNROLL = 20
READ_UNROLL = 8
TURN_UNROLL = 16
PADDING = max(MAKE_UNROLL, READ_UNROLL)
VMEM_LIMIT = 3 * 1024 * 1024


def hop(value, src_mask, tgt_mask=0):
    cores = lax.axis_size("tgt")
    total = lax.axis_size("src") * cores
    flip = src_mask * cores + tgt_mask
    return lax.ppermute(value, ("src", "tgt"), [(i, i ^ flip) for i in range(total)])


def half_norms(rows):
    wide = rows.astype(jnp.float32)
    return 0.5 * jnp.sum(wide * wide, axis=-1).reshape(-1, TILE)


def list_kernel(half, src_rows, own_cols, slots, own, peer, ids):
    position = lax.axis_index("src")
    upper = position // half
    col_blocks = half * own_cols
    late = ((position % half) ^ (half - 1)) * own_cols
    listed = own.shape[3]

    def scan(refs, shift, wanted):
        def step(k, found):
            col = refs[0, 0, 1, k] - upper * col_blocks
            ids[found] = refs[0, 0, 0, k] + shift * src_rows
            ids[slots + found] = col
            return found + wanted(col).astype(jnp.int32)

        return step

    def is_late(col):
        return (col >= late) & (col < late + own_cols)

    def is_here(col):
        return (col >= 0) & (col < col_blocks)

    early = scan(own, upper, lambda col: is_here(col) & jnp.logical_not(is_late(col)))
    found = lax.fori_loop(0, listed, early, 0, unroll=8)
    ids[2 * slots + 1] = found
    found = lax.fori_loop(0, listed, scan(own, upper, is_late), found, unroll=8)
    found = lax.fori_loop(0, listed, scan(peer, 1 - upper, is_here), found, unroll=8)
    for extra in range(PADDING):
        ids[found + extra] = 0
        ids[slots + found + extra] = 0
    ids[2 * slots] = found


def merge_logs(parts):
    peak = parts[0]
    for part in parts[1:]:
        peak = jnp.maximum(peak, part)
    return peak + jnp.log2(sum(jnp.exp2(part - peak) for part in parts))


def spread_out(potential, spread, begin=0):
    turned = jnp.transpose(potential)
    for block in range(potential.shape[0]):
        spread[begin + block] = jnp.broadcast_to(turned[:, block : block + 1], (TILE, TILE))


def clear(peaks, sums):
    peaks[...] = jnp.full(peaks.shape, FLOOR, jnp.float32)
    sums[...] = jnp.zeros(sums.shape, jnp.float32)


def sweep(unroll, begin, count, scores_of, known_of, reduced_of, spread, peaks, sums):
    dummy = peaks.shape[0] - 1

    def merge(carry):
        for place, peak, summed in carry:
            old_peak = peaks[place]
            old_sum = sums[place]
            top = jnp.maximum(old_peak, peak)
            peaks[place] = top
            sums[place] = old_sum * jnp.exp2(old_peak - top) + summed * jnp.exp2(peak - top)

    def turn(index, carry):
        merge(carry)
        fresh = []
        for lane in range(unroll):
            slot = begin + index * unroll + lane
            scores = (scores_of(slot) + spread[known_of(slot)]).reshape(TILE // 8, 8, TILE)
            peak = jnp.max(scores, axis=0)
            summed = jnp.sum(jnp.exp2(scores - peak[None]), axis=0)
            fresh.append((jnp.where(slot < count, reduced_of(slot), dummy), peak, summed))
        return tuple(fresh)

    nothing = tuple(
        (jnp.int32(dummy), jnp.full((8, TILE), FLOOR, jnp.float32), jnp.zeros((8, TILE), jnp.float32))
        for lane in range(unroll)
    )
    merge(lax.fori_loop(0, (count - begin + unroll - 1) // unroll, turn, nothing))


def log_sums(peaks, sums):
    top = peaks[0 : peaks.shape[0] - 1]
    peak = jnp.max(top, axis=1)
    summed = jnp.sum(sums[0 : top.shape[0]] * jnp.exp2(top - peak[:, None, :]), axis=1)
    live = summed > 0.0
    return jnp.where(live, peak + jnp.log2(jnp.where(live, summed, 1.0)), FLOOR)


def gather_parts(meta, groups, sems, first_sem):
    moves = []
    for pieces, places_of, whole in groups:
        for ref, place in zip(pieces, places_of):
            begin = pl.multiple_of(place(meta), ref.shape[0])
            moves.append(
                pltpu.make_async_copy(
                    ref, whole.at[pl.ds(begin, ref.shape[0])], sems.at[first_sem + len(moves)]
                )
            )
    return moves


def first_kernel(scale, half, slots, late, places, ids_any, start, *refs):
    n_src, n_tgt = places
    norm_parts, refs = refs[: len(n_tgt)], refs[len(n_tgt) :]
    src_pieces, refs = refs[: len(n_src)], refs[len(n_src) :]
    tgt_pieces, refs = refs[: len(n_tgt)], refs[len(n_tgt) :]
    if late:
        mass, out, refs = refs[0], refs[8], refs[9:]
    by_col, src, tgt, norms, spread, peaks, sums, ids, sems = refs
    position = lax.axis_index("src")
    meta = (position // half, lax.axis_index("tgt"), position % half)
    moves = [pltpu.make_async_copy(ids_any, ids, sems.at[0])]
    moves += gather_parts(meta, ((src_pieces, n_src, src), (tgt_pieces, n_tgt, tgt)), sems, 1)
    for move in moves:
        move.start()
    if not late:
        clear(peaks, sums)
    for ref, place in zip(norm_parts, n_tgt):
        begin = pl.multiple_of(place(meta), ref.shape[0])
        norms[pl.ds(begin, ref.shape[0])] = ref[...]
        spread_out(start[pl.ds(begin, ref.shape[0])] - scale * ref[...], spread, begin)
    for move in moves:
        move.wait()

    def scores_of(slot):
        products = scale * lax.dot_general(
            tgt[ids[slots + slot]],
            src[ids[slot]],
            (((1,), (1,)), ((), ())),
            preferred_element_type=jnp.float32,
        )
        by_col[jnp.minimum(slot, by_col.shape[0] - 1)] = products
        return products

    sweep(
        MAKE_UNROLL,
        ids[2 * slots + 1] if late else 0,
        ids[2 * slots] if late else ids[2 * slots + 1],
        scores_of,
        lambda slot: ids[slots + slot],
        lambda slot: ids[slot],
        spread,
        peaks,
        sums,
    )
    if late:
        own = mass.shape[0]
        out[0 : 2 * own] = log_sums(peaks, sums)
        out[2 * own :] = jnp.log2(mass[...])


def pass_kernel(half, slots, row_pass, n_parts, makes, has_out, ids_any, *refs):
    parts, refs = refs[:n_parts], refs[n_parts:]
    mass, refs = refs[0], refs[1:]
    if makes:
        turned, out, products, pair, refs = *refs[:4], refs[4:]
    else:
        products, out, refs = *refs[:2], refs[2:]
    if has_out:
        extra, refs = refs[0], refs[1:]
    ids, spread, peaks, sums, sem = refs
    move = pltpu.make_async_copy(ids_any, ids, sem)
    move.start()
    clear(peaks, sums)
    if makes:
        own = mass.shape[0] // 3
        upper = lax.axis_index("src") // half
        pair[pl.ds(pl.multiple_of(upper * own, own), own)] = mass[2 * own :]
        pair[pl.ds(pl.multiple_of((1 - upper) * own, own), own)] = parts[1][2 * own :]
        potential = pair[...] - merge_logs([part[0 : 2 * own] for part in parts])
    else:
        potential = mass[...] - merge_logs([part[...] for part in parts])
    if has_out:
        extra[...] = potential
    spread_out(potential, spread)
    move.wait()
    known, reduced = (slots, 0) if row_pass else (0, slots)

    def scores_of(slot):
        if not makes:
            return products[jnp.minimum(slot, products.shape[0] - 1)]
        place = jnp.minimum(slot, products.shape[0] - 1)
        made = jnp.transpose(turned[place])
        products[place] = made
        return made

    sweep(
        TURN_UNROLL if makes else READ_UNROLL,
        0,
        ids[2 * slots],
        scores_of,
        lambda slot: ids[known + slot],
        lambda slot: ids[reduced + slot],
        spread,
        peaks,
        sums,
    )
    out[...] = log_sums(peaks, sums)


def finish_kernel(scale, to_unit, parts_count, *refs):
    parts, (mass, norms, out) = refs[:parts_count], refs[parts_count:]
    potential = mass[...] - merge_logs([part[...] for part in parts])
    out[...] = (potential / scale + norms[...]) / to_unit


def shards(
    source_embed, target_embed, source_mass, target_mass, target_start, tile_list, tile_count
):
    width = source_embed.shape[1]
    shard_count = lax.axis_size("src")
    half = shard_count // 2
    src_index = lax.axis_index("src")
    upper = src_index // half
    scale = 2.0 / (width * EPSILON) * math.log2(math.e)
    to_unit = 0.5 * width

    source_blocks = source_embed.reshape(-1, TILE, width)
    target_blocks = target_embed.reshape(-1, TILE, width)
    src_rows = source_blocks.shape[0]
    own_cols = target_blocks.shape[0]
    col_blocks = own_cols * half
    side = src_rows // lax.axis_size("tgt")
    listed = tile_list.shape[3]
    slots = 2 * listed + PADDING

    smem = pl.BlockSpec(memory_space=pltpu.SMEM)
    vmem = pl.BlockSpec(memory_space=pltpu.VMEM)
    anywhere = pl.BlockSpec(memory_space=pl.ANY)
    params = pltpu.CompilerParams(vmem_limit_bytes=VMEM_LIMIT)

    def live_list(tiles, count):
        live = lax.broadcasted_iota(jnp.int32, tiles.shape, 3) < count[0, 0]
        return jnp.where(live, tiles, -1)

    share = lax.dynamic_slice_in_dim(source_blocks, lax.axis_index("tgt") * side, side)
    peer_count = hop(tile_count, half)
    sent_list, share = lax.optimization_barrier((tile_list, share))
    peer_list = hop(sent_list, half)
    direct = hop(share, half)
    held = {0: target_blocks}
    for slot in range(1, half):
        low = slot & -slot
        held[slot] = hop(held[slot ^ low], low)
    ids_size = -(-(2 * slots + 2) // 1024) * 1024
    ids = pl.pallas_call(
        lambda *refs: list_kernel(half, src_rows, own_cols, slots, *refs),
        out_shape=jax.ShapeDtypeStruct((ids_size,), jnp.int32),
        in_specs=[smem] * 2,
        out_specs=smem,
        compiler_params=params,
        name="tile_lists",
    )(live_list(tile_list, tile_count), live_list(peer_list, peer_count))
    ids_scratch = pltpu.SMEM((ids_size,), jnp.int32)

    log_half = jnp.log2(
        lax.dynamic_slice_in_dim(target_mass.reshape(-1, TILE), upper * col_blocks, col_blocks)
    )
    start = (scale * to_unit) * lax.dynamic_slice_in_dim(
        target_start.reshape(-1, TILE), upper * col_blocks, col_blocks
    )
    source_norms = half_norms(source_blocks)

    src_pieces = [source_blocks]
    src_places = [
        lambda meta: meta[0] * src_rows,
        lambda meta: (1 - meta[0]) * src_rows + meta[1] * side,
        lambda meta: (1 - meta[0]) * src_rows + (1 - meta[1]) * side,
    ]
    tgt_pieces, tgt_places, norm_parts = [], [], []
    for slot in range(half):
        tgt_pieces.append(held[slot])
        norm_parts.append(half_norms(held[slot]))
        tgt_places.append(lambda meta, slot=slot: (meta[2] ^ slot) * own_cols)

    def accumulators(known, reduced):
        return [
            ids_scratch,
            pltpu.VMEM((known, TILE, TILE), jnp.float32),
            pltpu.VMEM((reduced + 1, 8, TILE), jnp.float32),
            pltpu.VMEM((reduced + 1, 8, TILE), jnp.float32),
        ]

    shared = [
        jax.ShapeDtypeStruct((2 * listed + 1, TILE, TILE), jnp.float32),
        jax.ShapeDtypeStruct((2 * src_rows, TILE, width), jnp.bfloat16),
        jax.ShapeDtypeStruct((col_blocks, TILE, width), jnp.bfloat16),
        jax.ShapeDtypeStruct((col_blocks, TILE), jnp.float32),
        jax.ShapeDtypeStruct((col_blocks, TILE, TILE), jnp.float32),
        jax.ShapeDtypeStruct((2 * src_rows + 1, 8, TILE), jnp.float32),
        jax.ShapeDtypeStruct((2 * src_rows + 1, 8, TILE), jnp.float32),
    ]

    def first(late, given):
        srcs = slice(1, None) if late else slice(0, 1)
        tgts = slice(half - 1, None) if late else slice(0, half - 1)
        pieces = src_pieces[srcs] + tgt_pieces[tgts]
        norms = norm_parts[tgts]
        inputs = [ids, start, *norms, *pieces, *given]
        out_shape = shared
        if late:
            out_shape = [jax.ShapeDtypeStruct((3 * src_rows, TILE), jnp.float32)] + shared
        return pl.pallas_call(
            lambda *refs: first_kernel(
                scale, half, slots, late, (src_places[srcs], tgt_places[tgts]), *refs
            ),
            out_shape=out_shape,
            in_specs=[anywhere] + [vmem] * (1 + len(norms)) + [anywhere] * len(pieces) + [vmem] * len(given),
            out_specs=[vmem] * len(out_shape),
            scratch_shapes=[ids_scratch, pltpu.SemaphoreType.DMA((1 + len(pieces),))],
            input_output_aliases=(
                {len(inputs) - len(shared) + i: 1 + i for i in range(len(shared))} if late else {}
            ),
            compiler_params=params,
            name="late_row_pass" if late else "early_row_pass",
        )(*inputs)

    kept = list(first(False, []))
    direct, kept[5] = lax.optimization_barrier((direct, kept[5]))
    src_pieces[1:] = [direct, hop(direct, 0, 1)]
    rows, by_col, src, tgt, target_norms = first(
        True, [source_mass.reshape(src_rows, TILE), *kept]
    )[:5]

    def run(row_pass, parts, mass, products, makes, has_out):
        known, reduced = (col_blocks, 2 * src_rows) if row_pass else (2 * src_rows, col_blocks)
        out_shape = [jax.ShapeDtypeStruct((reduced, TILE), jnp.float32)]
        if makes:
            out_shape.append(jax.ShapeDtypeStruct((2 * listed + 1, TILE, TILE), jnp.float32))
            out_shape.append(jax.ShapeDtypeStruct((known, TILE), jnp.float32))
        if has_out:
            out_shape.append(jax.ShapeDtypeStruct((known, TILE), jnp.float32))
        return pl.pallas_call(
            lambda *refs: pass_kernel(half, slots, row_pass, len(parts), makes, has_out, *refs),
            out_shape=out_shape,
            in_specs=[anywhere] + [vmem] * (len(parts) + 2),
            out_specs=[vmem] * len(out_shape),
            scratch_shapes=accumulators(known, reduced) + [pltpu.SemaphoreType.DMA],
            compiler_params=params,
            name="row_pass" if row_pass else "column_pass",
        )(ids, *parts, mass, products)

    def share_rows(part):
        return [part, hop(part, half), hop(part, half, 1), hop(part, 0, 1)]

    def share_columns(part):
        return [part] + [hop(part, mask) for mask in range(1, half)]

    columns, by_row, log_pair = run(False, share_rows(rows), rows, by_col, True, False)
    rows = run(True, share_columns(columns), log_half, by_col, False, False)[0]
    columns, source_final = run(False, share_rows(rows), log_pair, by_row, False, True)
    gathered = share_columns(columns)
    target_final = pl.pallas_call(
        lambda *refs: finish_kernel(scale, to_unit, len(gathered), *refs),
        out_shape=jax.ShapeDtypeStruct((col_blocks, TILE), jnp.float32),
        in_specs=[vmem] * (len(gathered) + 2),
        out_specs=vmem,
        compiler_params=params,
        name="finish",
    )(*gathered, log_half, target_norms)
    other = hop(target_final, half)
    target_pot = jnp.where(
        upper == 0, jnp.concatenate([target_final, other]), jnp.concatenate([other, target_final])
    )
    own_final = lax.dynamic_slice_in_dim(source_final, upper * src_rows, src_rows)
    source_pot = (own_final / scale + source_norms) / to_unit
    return (source_pot.reshape(-1), target_pot.reshape(-1))


def solution(mesh):
    return jax.shard_map(
        shards,
        mesh=mesh,
        in_specs=(
            P(("groups", "src"), None),
            P(("groups", "tgt", "src"), None),
            P(("groups", "src")),
            P(("groups", "tgt")),
            P(("groups", "tgt")),
            P(("groups", "src"), "tgt", None, None),
            P(("groups", "src"), "tgt"),
        ),
        out_specs=(P(("groups", "src")), P(("groups", "tgt"))),
        check_vma=False,
    )
```

```python
import math

import jax
import jax.numpy as jnp
from jax import lax
from jax.experimental import pallas as pl
from jax.experimental.pallas import tpu as pltpu
from jax.sharding import PartitionSpec as P

TILE = 128
EPSILON = 0.05
FLOOR = -1e30
MAKE_UNROLL = 20
READ_UNROLL = 8
TURN_UNROLL = 16
PADDING = max(MAKE_UNROLL, READ_UNROLL)
VMEM_LIMIT = 3 * 1024 * 1024


def hop(value, src_mask, tgt_mask=0):
    cores = lax.axis_size("tgt")
    total = lax.axis_size("src") * cores
    flip = src_mask * cores + tgt_mask
    return lax.ppermute(value, ("src", "tgt"), [(i, i ^ flip) for i in range(total)])


def half_norms(rows):
    wide = rows.astype(jnp.float32)
    return 0.5 * jnp.sum(wide * wide, axis=-1).reshape(-1, TILE)


def list_kernel(half, src_rows, own_cols, slots, own, peer, ids):
    position = lax.axis_index("src")
    upper = position // half
    col_blocks = half * own_cols
    late = ((position % half) ^ (half - 1)) * own_cols
    listed = own.shape[3]

    def scan(refs, shift, wanted):
        def step(k, found):
            col = refs[0, 0, 1, k] - upper * col_blocks
            ids[found] = refs[0, 0, 0, k] + shift * src_rows
            ids[slots + found] = col
            return found + wanted(col).astype(jnp.int32)

        return step

    def is_late(col):
        return (col >= late) & (col < late + own_cols)

    def is_here(col):
        return (col >= 0) & (col < col_blocks)

    early = scan(own, upper, lambda col: is_here(col) & jnp.logical_not(is_late(col)))
    found = lax.fori_loop(0, listed, early, 0, unroll=8)
    ids[2 * slots + 1] = found
    found = lax.fori_loop(0, listed, scan(own, upper, is_late), found, unroll=8)
    found = lax.fori_loop(0, listed, scan(peer, 1 - upper, is_here), found, unroll=8)
    for extra in range(PADDING):
        ids[found + extra] = 0
        ids[slots + found + extra] = 0
    ids[2 * slots] = found


def merge_logs(parts):
    peak = parts[0]
    for part in parts[1:]:
        peak = jnp.maximum(peak, part)
    return peak + jnp.log2(sum(jnp.exp2(part - peak) for part in parts))


def spread_out(potential, spread, begin=0):
    turned = jnp.transpose(potential)
    for block in range(potential.shape[0]):
        spread[begin + block] = jnp.broadcast_to(turned[:, block : block + 1], (TILE, TILE))


def clear(peaks, sums):
    peaks[...] = jnp.full(peaks.shape, FLOOR, jnp.float32)
    sums[...] = jnp.zeros(sums.shape, jnp.float32)


def sweep(unroll, begin, count, scores_of, known_of, reduced_of, spread, peaks, sums):
    dummy = peaks.shape[0] - 1

    def merge(carry):
        for place, peak, summed in carry:
            old_peak = peaks[place]
            old_sum = sums[place]
            top = jnp.maximum(old_peak, peak)
            peaks[place] = top
            sums[place] = old_sum * jnp.exp2(old_peak - top) + summed * jnp.exp2(peak - top)

    def turn(index, carry):
        merge(carry)
        fresh = []
        for lane in range(unroll):
            slot = begin + index * unroll + lane
            scores = (scores_of(slot) + spread[known_of(slot)]).reshape(TILE // 8, 8, TILE)
            peak = jnp.max(scores, axis=0)
            summed = jnp.sum(jnp.exp2(scores - peak[None]), axis=0)
            fresh.append((jnp.where(slot < count, reduced_of(slot), dummy), peak, summed))
        return tuple(fresh)

    nothing = tuple(
        (jnp.int32(dummy), jnp.full((8, TILE), FLOOR, jnp.float32), jnp.zeros((8, TILE), jnp.float32))
        for lane in range(unroll)
    )
    merge(lax.fori_loop(0, (count - begin + unroll - 1) // unroll, turn, nothing))


def log_sums(peaks, sums):
    top = peaks[0 : peaks.shape[0] - 1]
    peak = jnp.max(top, axis=1)
    summed = jnp.sum(sums[0 : top.shape[0]] * jnp.exp2(top - peak[:, None, :]), axis=1)
    live = summed > 0.0
    return jnp.where(live, peak + jnp.log2(jnp.where(live, summed, 1.0)), FLOOR)


def gather_parts(meta, groups, sems, first_sem):
    moves = []
    for pieces, places_of, whole in groups:
        for ref, place in zip(pieces, places_of):
            begin = pl.multiple_of(place(meta), ref.shape[0])
            moves.append(
                pltpu.make_async_copy(
                    ref, whole.at[pl.ds(begin, ref.shape[0])], sems.at[first_sem + len(moves)]
                )
            )
    return moves


def first_kernel(scale, half, slots, late, places, ids_any, start, *refs):
    n_src, n_tgt = places
    norm_parts, refs = refs[: len(n_tgt)], refs[len(n_tgt) :]
    src_pieces, refs = refs[: len(n_src)], refs[len(n_src) :]
    tgt_pieces, refs = refs[: len(n_tgt)], refs[len(n_tgt) :]
    if late:
        mass, out, refs = refs[0], refs[8], refs[9:]
    by_col, src, tgt, norms, spread, peaks, sums, ids, sems = refs
    position = lax.axis_index("src")
    meta = (position // half, lax.axis_index("tgt"), position % half)
    moves = [pltpu.make_async_copy(ids_any, ids, sems.at[0])]
    moves += gather_parts(meta, ((src_pieces, n_src, src), (tgt_pieces, n_tgt, tgt)), sems, 1)
    for move in moves:
        move.start()
    if not late:
        clear(peaks, sums)
    for ref, place in zip(norm_parts, n_tgt):
        begin = pl.multiple_of(place(meta), ref.shape[0])
        norms[pl.ds(begin, ref.shape[0])] = ref[...]
        spread_out(start[pl.ds(begin, ref.shape[0])] - scale * ref[...], spread, begin)
    for move in moves:
        move.wait()

    def scores_of(slot):
        products = scale * lax.dot_general(
            tgt[ids[slots + slot]],
            src[ids[slot]],
            (((1,), (1,)), ((), ())),
            preferred_element_type=jnp.float32,
        )
        by_col[jnp.minimum(slot, by_col.shape[0] - 1)] = products
        return products

    sweep(
        MAKE_UNROLL,
        ids[2 * slots + 1] if late else 0,
        ids[2 * slots] if late else ids[2 * slots + 1],
        scores_of,
        lambda slot: ids[slots + slot],
        lambda slot: ids[slot],
        spread,
        peaks,
        sums,
    )
    if late:
        own = mass.shape[0]
        out[0 : 2 * own] = log_sums(peaks, sums)
        out[2 * own :] = jnp.log2(mass[...])


def pass_kernel(half, slots, row_pass, n_parts, makes, has_out, ids_any, *refs):
    parts, refs = refs[:n_parts], refs[n_parts:]
    mass, refs = refs[0], refs[1:]
    if makes:
        turned, out, products, pair, refs = *refs[:4], refs[4:]
    else:
        products, out, refs = *refs[:2], refs[2:]
    if has_out:
        extra, refs = refs[0], refs[1:]
    ids, spread, peaks, sums, sem = refs
    move = pltpu.make_async_copy(ids_any, ids, sem)
    move.start()
    clear(peaks, sums)
    if makes:
        own = mass.shape[0] // 3
        upper = lax.axis_index("src") // half
        pair[pl.ds(pl.multiple_of(upper * own, own), own)] = mass[2 * own :]
        pair[pl.ds(pl.multiple_of((1 - upper) * own, own), own)] = parts[1][2 * own :]
        potential = pair[...] - merge_logs([part[0 : 2 * own] for part in parts])
    else:
        potential = mass[...] - merge_logs([part[...] for part in parts])
    if has_out:
        extra[...] = potential
    spread_out(potential, spread)
    move.wait()
    known, reduced = (slots, 0) if row_pass else (0, slots)

    def scores_of(slot):
        if not makes:
            return products[jnp.minimum(slot, products.shape[0] - 1)]
        place = jnp.minimum(slot, products.shape[0] - 1)
        made = jnp.transpose(turned[place])
        products[place] = made
        return made

    sweep(
        TURN_UNROLL if makes else READ_UNROLL,
        0,
        ids[2 * slots],
        scores_of,
        lambda slot: ids[known + slot],
        lambda slot: ids[reduced + slot],
        spread,
        peaks,
        sums,
    )
    out[...] = log_sums(peaks, sums)


def finish_kernel(scale, to_unit, parts_count, *refs):
    parts, (mass, norms, out) = refs[:parts_count], refs[parts_count:]
    potential = mass[...] - merge_logs([part[...] for part in parts])
    out[...] = (potential / scale + norms[...]) / to_unit


def shards(
    source_embed, target_embed, source_mass, target_mass, target_start, tile_list, tile_count
):
    width = source_embed.shape[1]
    shard_count = lax.axis_size("src")
    half = shard_count // 2
    src_index = lax.axis_index("src")
    upper = src_index // half
    scale = 2.0 / (width * EPSILON) * math.log2(math.e)
    to_unit = 0.5 * width

    source_blocks = source_embed.reshape(-1, TILE, width)
    target_blocks = target_embed.reshape(-1, TILE, width)
    src_rows = source_blocks.shape[0]
    own_cols = target_blocks.shape[0]
    col_blocks = own_cols * half
    side = src_rows // lax.axis_size("tgt")
    listed = tile_list.shape[3]
    slots = 2 * listed + PADDING

    smem = pl.BlockSpec(memory_space=pltpu.SMEM)
    vmem = pl.BlockSpec(memory_space=pltpu.VMEM)
    anywhere = pl.BlockSpec(memory_space=pl.ANY)
    params = pltpu.CompilerParams(vmem_limit_bytes=VMEM_LIMIT)

    def live_list(tiles, count):
        live = lax.broadcasted_iota(jnp.int32, tiles.shape, 3) < count[0, 0]
        return jnp.where(live, tiles, -1)

    share = lax.dynamic_slice_in_dim(source_blocks, lax.axis_index("tgt") * side, side)
    peer_count = hop(tile_count, half)
    sent_list, share = lax.optimization_barrier((tile_list, share))
    peer_list = hop(sent_list, half)
    direct = hop(share, half)
    held = {0: target_blocks}
    for slot in range(1, half):
        low = slot & -slot
        held[slot] = hop(held[slot ^ low], low)
    ids_size = -(-(2 * slots + 2) // 1024) * 1024
    ids = pl.pallas_call(
        lambda *refs: list_kernel(half, src_rows, own_cols, slots, *refs),
        out_shape=jax.ShapeDtypeStruct((ids_size,), jnp.int32),
        in_specs=[smem] * 2,
        out_specs=smem,
        compiler_params=params,
        name="tile_lists",
    )(live_list(tile_list, tile_count), live_list(peer_list, peer_count))
    ids_scratch = pltpu.SMEM((ids_size,), jnp.int32)

    log_half = jnp.log2(
        lax.dynamic_slice_in_dim(target_mass.reshape(-1, TILE), upper * col_blocks, col_blocks)
    )
    start = (scale * to_unit) * lax.dynamic_slice_in_dim(
        target_start.reshape(-1, TILE), upper * col_blocks, col_blocks
    )
    source_norms = half_norms(source_blocks)

    src_pieces = [source_blocks]
    src_places = [
        lambda meta: meta[0] * src_rows,
        lambda meta: (1 - meta[0]) * src_rows + meta[1] * side,
        lambda meta: (1 - meta[0]) * src_rows + (1 - meta[1]) * side,
    ]
    tgt_pieces, tgt_places, norm_parts = [], [], []
    for slot in range(half):
        tgt_pieces.append(held[slot])
        norm_parts.append(half_norms(held[slot]))
        tgt_places.append(lambda meta, slot=slot: (meta[2] ^ slot) * own_cols)

    def accumulators(known, reduced):
        return [
            ids_scratch,
            pltpu.VMEM((known, TILE, TILE), jnp.float32),
            pltpu.VMEM((reduced + 1, 8, TILE), jnp.float32),
            pltpu.VMEM((reduced + 1, 8, TILE), jnp.float32),
        ]

    shared = [
        jax.ShapeDtypeStruct((2 * listed + 1, TILE, TILE), jnp.float32),
        jax.ShapeDtypeStruct((2 * src_rows, TILE, width), jnp.bfloat16),
        jax.ShapeDtypeStruct((col_blocks, TILE, width), jnp.bfloat16),
        jax.ShapeDtypeStruct((col_blocks, TILE), jnp.float32),
        jax.ShapeDtypeStruct((col_blocks, TILE, TILE), jnp.float32),
        jax.ShapeDtypeStruct((2 * src_rows + 1, 8, TILE), jnp.float32),
        jax.ShapeDtypeStruct((2 * src_rows + 1, 8, TILE), jnp.float32),
    ]

    def first(late, given):
        srcs = slice(1, None) if late else slice(0, 1)
        tgts = slice(half - 1, None) if late else slice(0, half - 1)
        pieces = src_pieces[srcs] + tgt_pieces[tgts]
        norms = norm_parts[tgts]
        inputs = [ids, start, *norms, *pieces, *given]
        out_shape = shared
        if late:
            out_shape = [jax.ShapeDtypeStruct((3 * src_rows, TILE), jnp.float32)] + shared
        return pl.pallas_call(
            lambda *refs: first_kernel(
                scale, half, slots, late, (src_places[srcs], tgt_places[tgts]), *refs
            ),
            out_shape=out_shape,
            in_specs=[anywhere] + [vmem] * (1 + len(norms)) + [anywhere] * len(pieces) + [vmem] * len(given),
            out_specs=[vmem] * len(out_shape),
            scratch_shapes=[ids_scratch, pltpu.SemaphoreType.DMA((1 + len(pieces),))],
            input_output_aliases=(
                {len(inputs) - len(shared) + i: 1 + i for i in range(len(shared))} if late else {}
            ),
            compiler_params=params,
            name="late_row_pass" if late else "early_row_pass",
        )(*inputs)

    kept = list(first(False, []))
    direct, kept[5] = lax.optimization_barrier((direct, kept[5]))
    src_pieces[1:] = [direct, hop(direct, 0, 1)]
    rows, by_col, src, tgt, target_norms = first(
        True, [source_mass.reshape(src_rows, TILE), *kept]
    )[:5]

    def run(row_pass, parts, mass, products, makes, has_out):
        known, reduced = (col_blocks, 2 * src_rows) if row_pass else (2 * src_rows, col_blocks)
        out_shape = [jax.ShapeDtypeStruct((reduced, TILE), jnp.float32)]
        if makes:
            out_shape.append(jax.ShapeDtypeStruct((2 * listed + 1, TILE, TILE), jnp.float32))
            out_shape.append(jax.ShapeDtypeStruct((known, TILE), jnp.float32))
        if has_out:
            out_shape.append(jax.ShapeDtypeStruct((known, TILE), jnp.float32))
        return pl.pallas_call(
            lambda *refs: pass_kernel(half, slots, row_pass, len(parts), makes, has_out, *refs),
            out_shape=out_shape,
            in_specs=[anywhere] + [vmem] * (len(parts) + 2),
            out_specs=[vmem] * len(out_shape),
            scratch_shapes=accumulators(known, reduced) + [pltpu.SemaphoreType.DMA],
            compiler_params=params,
            name="row_pass" if row_pass else "column_pass",
        )(ids, *parts, mass, products)

    def share_rows(part):
        return [part, hop(part, half), hop(part, half, 1), hop(part, 0, 1)]

    def share_columns(part):
        return [part] + [hop(part, mask) for mask in reversed(range(1, half))]

    columns, by_row, log_pair = run(False, share_rows(rows), rows, by_col, True, False)
    rows = run(True, share_columns(columns), log_half, by_col, False, False)[0]
    columns, source_final = run(False, share_rows(rows), log_pair, by_row, False, True)
    gathered = share_columns(columns)
    target_final = pl.pallas_call(
        lambda *refs: finish_kernel(scale, to_unit, len(gathered), *refs),
        out_shape=jax.ShapeDtypeStruct((col_blocks, TILE), jnp.float32),
        in_specs=[vmem] * (len(gathered) + 2),
        out_specs=vmem,
        compiler_params=params,
        name="finish",
    )(*gathered, log_half, target_norms)
    other = hop(target_final, half)
    target_pot = jnp.where(
        upper == 0, jnp.concatenate([target_final, other]), jnp.concatenate([other, target_final])
    )
    own_final = lax.dynamic_slice_in_dim(source_final, upper * src_rows, src_rows)
    source_pot = (own_final / scale + source_norms) / to_unit
    return (source_pot.reshape(-1), target_pot.reshape(-1))


def solution(mesh):
    return jax.shard_map(
        shards,
        mesh=mesh,
        in_specs=(
            P(("groups", "src"), None),
            P(("groups", "tgt", "src"), None),
            P(("groups", "src")),
            P(("groups", "tgt")),
            P(("groups", "tgt")),
            P(("groups", "src"), "tgt", None, None),
            P(("groups", "src"), "tgt"),
        ),
        out_specs=(P(("groups", "src")), P(("groups", "tgt"))),
        check_vma=False,
    )
```

```python
import math

import jax
import jax.numpy as jnp
from jax import lax
from jax.experimental import pallas as pl
from jax.experimental.pallas import tpu as pltpu
from jax.sharding import PartitionSpec as P

TILE = 128
EPSILON = 0.05
FLOOR = -1e30
MAKE_UNROLL = 20
READ_UNROLL = 8
TURN_UNROLL = 20
PADDING = max(MAKE_UNROLL, READ_UNROLL, TURN_UNROLL)
VMEM_LIMIT = 3 * 1024 * 1024


def hop(value, src_mask, tgt_mask=0):
    cores = lax.axis_size("tgt")
    total = lax.axis_size("src") * cores
    flip = src_mask * cores + tgt_mask
    return lax.ppermute(value, ("src", "tgt"), [(i, i ^ flip) for i in range(total)])


def half_norms(rows):
    wide = rows.astype(jnp.float32)
    return 0.5 * jnp.sum(wide * wide, axis=-1).reshape(-1, TILE)


def list_kernel(half, src_rows, own_cols, slots, own, peer, ids):
    position = lax.axis_index("src")
    upper = position // half
    col_blocks = half * own_cols
    late = ((position % half) ^ (half - 1)) * own_cols
    listed = own.shape[3]

    def scan(refs, shift, wanted):
        def step(k, found):
            col = refs[0, 0, 1, k] - upper * col_blocks
            ids[found] = refs[0, 0, 0, k] + shift * src_rows
            ids[slots + found] = col
            return found + wanted(col).astype(jnp.int32)

        return step

    def is_late(col):
        return (col >= late) & (col < late + own_cols)

    def is_here(col):
        return (col >= 0) & (col < col_blocks)

    early = scan(own, upper, lambda col: is_here(col) & jnp.logical_not(is_late(col)))
    found = lax.fori_loop(0, listed, early, 0, unroll=8)
    ids[2 * slots + 1] = found
    found = lax.fori_loop(0, listed, scan(own, upper, is_late), found, unroll=8)
    found = lax.fori_loop(0, listed, scan(peer, 1 - upper, is_here), found, unroll=8)
    for extra in range(PADDING):
        ids[found + extra] = 0
        ids[slots + found + extra] = 0
    ids[2 * slots] = found


def merge_logs(parts):
    peak = parts[0]
    for part in parts[1:]:
        peak = jnp.maximum(peak, part)
    return peak + jnp.log2(sum(jnp.exp2(part - peak) for part in parts))


def spread_out(potential, spread, begin=0):
    turned = jnp.transpose(potential)
    for block in range(potential.shape[0]):
        spread[begin + block] = jnp.broadcast_to(turned[:, block : block + 1], (TILE, TILE))


def clear(peaks, sums):
    peaks[...] = jnp.full(peaks.shape, FLOOR, jnp.float32)
    sums[...] = jnp.zeros(sums.shape, jnp.float32)


def sweep(unroll, begin, count, scores_of, known_of, reduced_of, spread, peaks, sums):
    dummy = peaks.shape[0] - 1

    def merge(carry):
        for place, peak, summed in carry:
            old_peak = peaks[place]
            old_sum = sums[place]
            top = jnp.maximum(old_peak, peak)
            peaks[place] = top
            sums[place] = old_sum * jnp.exp2(old_peak - top) + summed * jnp.exp2(peak - top)

    def turn(index, carry):
        merge(carry)
        fresh = []
        for lane in range(unroll):
            slot = begin + index * unroll + lane
            scores = (scores_of(slot) + spread[known_of(slot)]).reshape(TILE // 8, 8, TILE)
            peak = jnp.max(scores, axis=0)
            summed = jnp.sum(jnp.exp2(scores - peak[None]), axis=0)
            fresh.append((jnp.where(slot < count, reduced_of(slot), dummy), peak, summed))
        return tuple(fresh)

    nothing = tuple(
        (jnp.int32(dummy), jnp.full((8, TILE), FLOOR, jnp.float32), jnp.zeros((8, TILE), jnp.float32))
        for lane in range(unroll)
    )
    merge(lax.fori_loop(0, (count - begin + unroll - 1) // unroll, turn, nothing))


def log_sums(peaks, sums):
    top = peaks[0 : peaks.shape[0] - 1]
    peak = jnp.max(top, axis=1)
    summed = jnp.sum(sums[0 : top.shape[0]] * jnp.exp2(top - peak[:, None, :]), axis=1)
    live = summed > 0.0
    return jnp.where(live, peak + jnp.log2(jnp.where(live, summed, 1.0)), FLOOR)


def gather_parts(meta, groups, sems, first_sem):
    moves = []
    for pieces, places_of, whole in groups:
        for ref, place in zip(pieces, places_of):
            begin = pl.multiple_of(place(meta), ref.shape[0])
            moves.append(
                pltpu.make_async_copy(
                    ref, whole.at[pl.ds(begin, ref.shape[0])], sems.at[first_sem + len(moves)]
                )
            )
    return moves


def first_kernel(scale, half, slots, late, places, ids_any, start, *refs):
    n_src, n_tgt = places
    norm_parts, refs = refs[: len(n_tgt)], refs[len(n_tgt) :]
    src_pieces, refs = refs[: len(n_src)], refs[len(n_src) :]
    tgt_pieces, refs = refs[: len(n_tgt)], refs[len(n_tgt) :]
    if late:
        mass, out, refs = refs[0], refs[8], refs[9:]
    by_col, src, tgt, norms, spread, peaks, sums, ids, sems = refs
    position = lax.axis_index("src")
    meta = (position // half, lax.axis_index("tgt"), position % half)
    moves = [pltpu.make_async_copy(ids_any, ids, sems.at[0])]
    moves += gather_parts(meta, ((src_pieces, n_src, src), (tgt_pieces, n_tgt, tgt)), sems, 1)
    for move in moves:
        move.start()
    if not late:
        clear(peaks, sums)
    for ref, place in zip(norm_parts, n_tgt):
        begin = pl.multiple_of(place(meta), ref.shape[0])
        norms[pl.ds(begin, ref.shape[0])] = ref[...]
        spread_out(start[pl.ds(begin, ref.shape[0])] - scale * ref[...], spread, begin)
    for move in moves:
        move.wait()

    def scores_of(slot):
        products = scale * lax.dot_general(
            tgt[ids[slots + slot]],
            src[ids[slot]],
            (((1,), (1,)), ((), ())),
            preferred_element_type=jnp.float32,
        )
        by_col[jnp.minimum(slot, by_col.shape[0] - 1)] = products
        return products

    sweep(
        MAKE_UNROLL,
        ids[2 * slots + 1] if late else 0,
        ids[2 * slots] if late else ids[2 * slots + 1],
        scores_of,
        lambda slot: ids[slots + slot],
        lambda slot: ids[slot],
        spread,
        peaks,
        sums,
    )
    if late:
        own = mass.shape[0]
        out[0 : 2 * own] = log_sums(peaks, sums)
        out[2 * own :] = jnp.log2(mass[...])


def pass_kernel(half, slots, row_pass, n_parts, makes, has_out, ids_any, *refs):
    parts, refs = refs[:n_parts], refs[n_parts:]
    mass, refs = refs[0], refs[1:]
    if makes:
        turned, out, products, pair, refs = *refs[:4], refs[4:]
    else:
        products, out, refs = *refs[:2], refs[2:]
    if has_out:
        extra, refs = refs[0], refs[1:]
    ids, spread, peaks, sums, sem = refs
    move = pltpu.make_async_copy(ids_any, ids, sem)
    move.start()
    clear(peaks, sums)
    if makes:
        own = mass.shape[0] // 3
        upper = lax.axis_index("src") // half
        pair[pl.ds(pl.multiple_of(upper * own, own), own)] = mass[2 * own :]
        pair[pl.ds(pl.multiple_of((1 - upper) * own, own), own)] = parts[1][2 * own :]
        potential = pair[...] - merge_logs([part[0 : 2 * own] for part in parts])
    else:
        potential = mass[...] - merge_logs([part[...] for part in parts])
    if has_out:
        extra[...] = potential
    spread_out(potential, spread)
    move.wait()
    known, reduced = (slots, 0) if row_pass else (0, slots)

    def scores_of(slot):
        if not makes:
            return products[jnp.minimum(slot, products.shape[0] - 1)]
        place = jnp.minimum(slot, products.shape[0] - 1)
        made = jnp.transpose(turned[place])
        products[place] = made
        return made

    sweep(
        TURN_UNROLL if makes else READ_UNROLL,
        0,
        ids[2 * slots],
        scores_of,
        lambda slot: ids[known + slot],
        lambda slot: ids[reduced + slot],
        spread,
        peaks,
        sums,
    )
    out[...] = log_sums(peaks, sums)


def finish_kernel(scale, to_unit, parts_count, *refs):
    parts, (mass, norms, out) = refs[:parts_count], refs[parts_count:]
    potential = mass[...] - merge_logs([part[...] for part in parts])
    out[...] = (potential / scale + norms[...]) / to_unit


def shards(
    source_embed, target_embed, source_mass, target_mass, target_start, tile_list, tile_count
):
    width = source_embed.shape[1]
    shard_count = lax.axis_size("src")
    half = shard_count // 2
    src_index = lax.axis_index("src")
    upper = src_index // half
    scale = 2.0 / (width * EPSILON) * math.log2(math.e)
    to_unit = 0.5 * width

    source_blocks = source_embed.reshape(-1, TILE, width)
    target_blocks = target_embed.reshape(-1, TILE, width)
    src_rows = source_blocks.shape[0]
    own_cols = target_blocks.shape[0]
    col_blocks = own_cols * half
    side = src_rows // lax.axis_size("tgt")
    listed = tile_list.shape[3]
    slots = 2 * listed + PADDING

    smem = pl.BlockSpec(memory_space=pltpu.SMEM)
    vmem = pl.BlockSpec(memory_space=pltpu.VMEM)
    anywhere = pl.BlockSpec(memory_space=pl.ANY)
    params = pltpu.CompilerParams(vmem_limit_bytes=VMEM_LIMIT)

    def live_list(tiles, count):
        live = lax.broadcasted_iota(jnp.int32, tiles.shape, 3) < count[0, 0]
        return jnp.where(live, tiles, -1)

    share = lax.dynamic_slice_in_dim(source_blocks, lax.axis_index("tgt") * side, side)
    peer_count = hop(tile_count, half)
    sent_list, share = lax.optimization_barrier((tile_list, share))
    peer_list = hop(sent_list, half)
    direct = hop(share, half)
    held = {0: target_blocks}
    for slot in range(1, half):
        low = slot & -slot
        held[slot] = hop(held[slot ^ low], low)
    ids_size = -(-(2 * slots + 2) // 1024) * 1024
    ids = pl.pallas_call(
        lambda *refs: list_kernel(half, src_rows, own_cols, slots, *refs),
        out_shape=jax.ShapeDtypeStruct((ids_size,), jnp.int32),
        in_specs=[smem] * 2,
        out_specs=smem,
        compiler_params=params,
        name="tile_lists",
    )(live_list(tile_list, tile_count), live_list(peer_list, peer_count))
    ids_scratch = pltpu.SMEM((ids_size,), jnp.int32)

    log_half = jnp.log2(
        lax.dynamic_slice_in_dim(target_mass.reshape(-1, TILE), upper * col_blocks, col_blocks)
    )
    start = (scale * to_unit) * lax.dynamic_slice_in_dim(
        target_start.reshape(-1, TILE), upper * col_blocks, col_blocks
    )
    source_norms = half_norms(source_blocks)

    src_pieces = [source_blocks]
    src_places = [
        lambda meta: meta[0] * src_rows,
        lambda meta: (1 - meta[0]) * src_rows + meta[1] * side,
        lambda meta: (1 - meta[0]) * src_rows + (1 - meta[1]) * side,
    ]
    tgt_pieces, tgt_places, norm_parts = [], [], []
    for slot in range(half):
        tgt_pieces.append(held[slot])
        norm_parts.append(half_norms(held[slot]))
        tgt_places.append(lambda meta, slot=slot: (meta[2] ^ slot) * own_cols)

    def accumulators(known, reduced):
        return [
            ids_scratch,
            pltpu.VMEM((known, TILE, TILE), jnp.float32),
            pltpu.VMEM((reduced + 1, 8, TILE), jnp.float32),
            pltpu.VMEM((reduced + 1, 8, TILE), jnp.float32),
        ]

    shared = [
        jax.ShapeDtypeStruct((2 * listed + 1, TILE, TILE), jnp.float32),
        jax.ShapeDtypeStruct((2 * src_rows, TILE, width), jnp.bfloat16),
        jax.ShapeDtypeStruct((col_blocks, TILE, width), jnp.bfloat16),
        jax.ShapeDtypeStruct((col_blocks, TILE), jnp.float32),
        jax.ShapeDtypeStruct((col_blocks, TILE, TILE), jnp.float32),
        jax.ShapeDtypeStruct((2 * src_rows + 1, 8, TILE), jnp.float32),
        jax.ShapeDtypeStruct((2 * src_rows + 1, 8, TILE), jnp.float32),
    ]

    def first(late, given):
        srcs = slice(1, None) if late else slice(0, 1)
        tgts = slice(half - 1, None) if late else slice(0, half - 1)
        pieces = src_pieces[srcs] + tgt_pieces[tgts]
        norms = norm_parts[tgts]
        inputs = [ids, start, *norms, *pieces, *given]
        out_shape = shared
        if late:
            out_shape = [jax.ShapeDtypeStruct((3 * src_rows, TILE), jnp.float32)] + shared
        return pl.pallas_call(
            lambda *refs: first_kernel(
                scale, half, slots, late, (src_places[srcs], tgt_places[tgts]), *refs
            ),
            out_shape=out_shape,
            in_specs=[anywhere] + [vmem] * (1 + len(norms)) + [anywhere] * len(pieces) + [vmem] * len(given),
            out_specs=[vmem] * len(out_shape),
            scratch_shapes=[ids_scratch, pltpu.SemaphoreType.DMA((1 + len(pieces),))],
            input_output_aliases=(
                {len(inputs) - len(shared) + i: 1 + i for i in range(len(shared))} if late else {}
            ),
            compiler_params=params,
            name="late_row_pass" if late else "early_row_pass",
        )(*inputs)

    kept = list(first(False, []))
    direct, kept[5] = lax.optimization_barrier((direct, kept[5]))
    src_pieces[1:] = [direct, hop(direct, 0, 1)]
    rows, by_col, src, tgt, target_norms = first(
        True, [source_mass.reshape(src_rows, TILE), *kept]
    )[:5]

    def run(row_pass, parts, mass, products, makes, has_out):
        known, reduced = (col_blocks, 2 * src_rows) if row_pass else (2 * src_rows, col_blocks)
        out_shape = [jax.ShapeDtypeStruct((reduced, TILE), jnp.float32)]
        if makes:
            out_shape.append(jax.ShapeDtypeStruct((2 * listed + 1, TILE, TILE), jnp.float32))
            out_shape.append(jax.ShapeDtypeStruct((known, TILE), jnp.float32))
        if has_out:
            out_shape.append(jax.ShapeDtypeStruct((known, TILE), jnp.float32))
        return pl.pallas_call(
            lambda *refs: pass_kernel(half, slots, row_pass, len(parts), makes, has_out, *refs),
            out_shape=out_shape,
            in_specs=[anywhere] + [vmem] * (len(parts) + 2),
            out_specs=[vmem] * len(out_shape),
            scratch_shapes=accumulators(known, reduced) + [pltpu.SemaphoreType.DMA],
            compiler_params=params,
            name="row_pass" if row_pass else "column_pass",
        )(ids, *parts, mass, products)

    def share_rows(part):
        return [part, hop(part, half), hop(part, half, 1), hop(part, 0, 1)]

    def share_columns(part):
        return [part] + [hop(part, mask) for mask in reversed(range(1, half))]

    columns, by_row, log_pair = run(False, share_rows(rows), rows, by_col, True, False)
    rows = run(True, share_columns(columns), log_half, by_col, False, False)[0]
    columns, source_final = run(False, share_rows(rows), log_pair, by_row, False, True)
    gathered = share_columns(columns)
    target_final = pl.pallas_call(
        lambda *refs: finish_kernel(scale, to_unit, len(gathered), *refs),
        out_shape=jax.ShapeDtypeStruct((col_blocks, TILE), jnp.float32),
        in_specs=[vmem] * (len(gathered) + 2),
        out_specs=vmem,
        compiler_params=params,
        name="finish",
    )(*gathered, log_half, target_norms)
    other = hop(target_final, half)
    target_pot = jnp.where(
        upper == 0, jnp.concatenate([target_final, other]), jnp.concatenate([other, target_final])
    )
    own_final = lax.dynamic_slice_in_dim(source_final, upper * src_rows, src_rows)
    source_pot = (own_final / scale + source_norms) / to_unit
    return (source_pot.reshape(-1), target_pot.reshape(-1))


def solution(mesh):
    return jax.shard_map(
        shards,
        mesh=mesh,
        in_specs=(
            P(("groups", "src"), None),
            P(("groups", "tgt", "src"), None),
            P(("groups", "src")),
            P(("groups", "tgt")),
            P(("groups", "tgt")),
            P(("groups", "src"), "tgt", None, None),
            P(("groups", "src"), "tgt"),
        ),
        out_specs=(P(("groups", "src")), P(("groups", "tgt"))),
        check_vma=False,
    )
```
